32 devices in a mesh: ta: 8 (over y, x, core), gx: 4 (over z).
Axes of the slice: x: 2, y: 2, z: 4, core: 2. Of those that a mesh axis runs over, the one named last changes fastest.
Arguments:
- eigenvectors: bfloat16 [16, 2, 32768, 3, 192], P('ta', None, 'gx'), may hold values from -6 to 6
- site_index: int32 [32768], P('gx'), may hold values from 0 to 32767, each once
- momenta: int32 [2, 3], replicated, may hold values from -3 to 3
- perambulators: bfloat16 [2, 16, 16, 768, 768], P(None, 'gx', 'ta'), may hold values from -6 to 6
- spin_perm: int32 [2, 4], replicated, may hold values from 0 to 3, each once within a row
- spin_sign: int32 [2, 4], replicated, may hold values from 0 to 1
Outputs:
- forward_box: bfloat16 [2, 16, 16, 768, 768], P(None, 'gx', 'ta')
- backward_box: bfloat16 [2, 16, 16, 768, 768], P(None, 'gx', 'ta')
The draws below stay inside these ranges and needn't reach their ends.
Inputs may be any that keep to these rules, and one draw needn't show every extreme that they name: `site_index`: each lattice site appears exactly once. `spin_perm`: each row is a permutation of the spins.
All inputs are finite; a program needn't handle non-finite values.
Results may differ from the reference program's by a relative error of at most 0.008.
Values may be sent and summed in bfloat16 or wider, within the bound.
No kernel may reach another device: no remote copies, remote signals or barrier semaphores. Data moves between devices by JAX's collectives and lax.ppermute only.
A program may use at most 256 MiB of HBM per device.

```python
import math
import jax
import jax.numpy as jnp
from jax import lax

L = 32
NT = 16
NEV = 192
COLOR = 3
SPIN = 4
MOMENTA = 2
SITES = 32768
NDIM = 768


def touch_ends(drawn, rng, least, top_value):
    spot = [jax.random.randint(jax.random.fold_in(rng, axis), (), 0, length) for axis, length in enumerate(drawn.shape)]
    widest = drawn.shape.index(max(drawn.shape))
    next_to = spot[:widest] + [(spot[widest] + 1) % drawn.shape[widest]] + spot[widest + 1:]
    return drawn.at[tuple(spot)].set(least).at[tuple(next_to)].set(top_value)


def levels(own_key, extent, cuts, smallest, largest):
    factor_of = 1.0
    for position, blocks in cuts:
        draws = jax.random.uniform(jax.random.fold_in(jax.random.fold_in(own_key, 6), position), (blocks,), jnp.float32, smallest / len(cuts), largest / len(cuts))
        factor_of = factor_of * jnp.repeat(jnp.exp(draws), extent[position] // blocks).reshape((-1,) + (1,) * (len(extent) - 1 - position))
    return factor_of


def gaussian(rng, extent, width, bound, split=(), kind=jnp.bfloat16):
    array = width * jax.random.normal(rng, extent, jnp.float32)
    if split:
        array = array * levels(rng, extent, split, -0.22, 0.18)
    return jnp.clip(array, -bound, bound).astype(kind)


def setup_inputs(seed: int = 0) -> dict:
    seeds = jax.random.split(jax.random.key(seed), 7)
    eigenvectors = gaussian(seeds[0], (NT, 2, SITES, COLOR, NEV), 1.0, 6.0, ((0, 8), (2, 4)))
    site_index = jax.random.permutation(seeds[1], SITES).astype(jnp.int32)
    momenta = touch_ends(jax.random.randint(seeds[2], (MOMENTA, 3), -3, 4), jax.random.fold_in(seeds[2], 1), -3, 3).astype(jnp.int32)
    perambulators = gaussian(seeds[3], (2, NT, NT, NDIM, NDIM), 1.0, 6.0, ((1, 4), (2, 8)))
    spin_perm = jax.vmap(lambda own: jax.random.permutation(own, SPIN))(jax.random.split(seeds[4], MOMENTA)).reshape((MOMENTA, SPIN)).astype(jnp.int32)
    spin_sign = touch_ends(jax.random.randint(seeds[5], (MOMENTA, SPIN), 0, 2), jax.random.fold_in(seeds[5], 1), 0, 1).astype(jnp.int32)
    return {"eigenvectors": eigenvectors, "site_index": site_index, "momenta": momenta, "perambulators": perambulators, "spin_perm": spin_perm, "spin_sign": spin_sign}


def phases(site_index, momenta):
    first_coord = site_index // (L * L)
    second = site_index // L % L
    third_coord = site_index % L
    dotted = momenta[:, 0:1] * first_coord[None, :] + momenta[:, 1:2] * second[None, :] + momenta[:, 2:3] * third_coord[None, :]
    angles = jnp.mod(dotted, L).astype(jnp.float32) * (2.0 * math.pi / L)
    return (jnp.cos(angles), jnp.sin(angles))

def inner_rows(first_op, second_op):
    return lax.dot_general(first_op, second_op, (((0, 1), (0, 1)), ((), ())), preferred_element_type=jnp.float32)

def project(vectors, cosine, sine_value):
    real_part = vectors[0].astype(jnp.float32)
    imag_part = vectors[1].astype(jnp.float32)
    results = []
    for momentum in range(cosine.shape[0]):
        cosine_now = cosine[momentum][:, None, None]
        sine_now = sine_value[momentum][:, None, None]
        turned_real = (cosine_now * real_part - sine_now * imag_part).astype(jnp.bfloat16)
        turned_imag = (cosine_now * imag_part + sine_now * real_part).astype(jnp.bfloat16)
        real_out = inner_rows(vectors[0], turned_real) + inner_rows(vectors[1], turned_imag)
        imag_out = inner_rows(vectors[0], turned_imag) - inner_rows(vectors[1], turned_real)
        results.append(jnp.stack([real_out, imag_out]))
    return jnp.stack(results)

def spin_tables(spin_perm, spin_sign):
    spin_count = spin_perm.shape[1]
    matches = (spin_perm[:, :, None] == jnp.arange(spin_count, dtype=jnp.int32)[None, None, :]).astype(jnp.float32)
    return matches * (2 * spin_sign - 1).astype(jnp.float32)[:, :, None]

def contract(form, first_op, second_op):
    return jnp.einsum(form, first_op.astype(jnp.float32), second_op.astype(jnp.float32))

def complex_table(matrix):
    return jnp.stack([jnp.stack([matrix[0], -matrix[1]]), jnp.stack([matrix[1], matrix[0]])])

def pair_blocks(peram_block, sink_elems, source_elems, tables):
    spin_count = tables.shape[1]
    vector_count = sink_elems.shape[-1]
    dimension = spin_count * vector_count
    chiral = jnp.where(jnp.arange(spin_count) < spin_count // 2, 1.0, -1.0).astype(jnp.float32)
    blocks = peram_block.reshape(2, spin_count, vector_count, dimension)
    stacked = []
    for first_vertex, second_vertex in ((0, 1), (1, 0)):
        mixed_rows = contract('rs,cslj->crlj', tables[first_vertex].astype(jnp.bfloat16), blocks).astype(jnp.bfloat16)
        left_side = contract('ockl,cslj->oskj', complex_table(sink_elems[first_vertex]), mixed_rows).astype(jnp.bfloat16)
        left_side = left_side.reshape(2, dimension, spin_count, vector_count)
        signed = (tables[second_vertex] * chiral[None, :]).astype(jnp.bfloat16)
        turned = contract('cisk,sr->cirk', left_side, signed).astype(jnp.bfloat16)
        product = contract('cisk,ockl->oisl', turned, complex_table(source_elems[second_vertex])).astype(jnp.bfloat16)
        product = product.reshape(2, dimension, dimension)
        stacked.append(jnp.stack([product, jnp.stack([product[1], -product[0]])]))
    both_ways = jnp.stack(stacked)
    closed = contract('docim,cjm->doij', both_ways, peram_block)
    weights = jnp.repeat(chiral, vector_count) * (0.5 / math.sqrt(dimension))
    return (closed * weights).astype(jnp.bfloat16)

def reference(eigenvectors, site_index, momenta, perambulators, spin_perm, spin_sign):
    cosine, sine_value = phases(site_index, momenta)
    norm_factor = 0.5 / math.sqrt(COLOR * SITES * NEV)

    def one_time(vectors):
        return (project(vectors, cosine, sine_value) * norm_factor).astype(jnp.bfloat16)
    elementals = lax.map(one_time, eigenvectors)
    tables = spin_tables(spin_perm, spin_sign)

    def one_pair(pair_index):
        sink_time = pair_index // NT
        source_time = pair_index % NT
        peram_block = perambulators[:, sink_time, source_time]
        return pair_blocks(peram_block, elementals[sink_time], elementals[source_time], tables)
    blocks = lax.map(one_pair, jnp.arange(NT * NT, dtype=jnp.int32))
    blocks = blocks.reshape(NT, NT, 2, 2, NDIM, NDIM).transpose(2, 3, 0, 1, 4, 5)
    return (blocks[0], blocks[1])
```

```python
import functools
import math

import jax
import jax.numpy as jnp
import numpy as np
from jax import lax
from jax.experimental import pallas as pl
from jax.experimental.pallas import tpu as pltpu
from jax.sharding import PartitionSpec as P

F32, BF16 = jnp.float32, jnp.bfloat16
L = 32
VMEM_LIMIT = 58 * 2**20
BOTH_LAST = (((1,), (1,)), ((), ()))


def phases(site_index, momenta):
    first_coord = site_index // (L * L)
    second = site_index // L % L
    third_coord = site_index % L
    dotted = (
        momenta[:, 0:1] * first_coord[None, :]
        + momenta[:, 1:2] * second[None, :]
        + momenta[:, 2:3] * third_coord[None, :]
    )
    angles = jnp.mod(dotted, L).astype(F32) * (2.0 * math.pi / L)
    return (jnp.cos(angles), jnp.sin(angles))


def rows_dot(a, b):
    return jnp.dot(a, b, preferred_element_type=F32)


def cols_dot(a, b):
    return lax.dot_general(a, b, BOTH_LAST, preferred_element_type=F32)


def elemental_kernel(scale, sub, shares, here_ref, cos_ref, sin_ref, v_ref, *refs):
    outs, (acc, flat), turned = refs[:shares], refs[shares : shares + 2], refs[shares + 2 :]
    step = pl.program_id(0)
    nev, span = v_ref.shape[3], v_ref.shape[4]

    def turn(j, into):
        at = pl.ds(j * sub, sub)
        vr = v_ref[0, 0, 0, :, at].astype(F32)
        vi = v_ref[0, 1, 0, :, at].astype(F32)
        for p in range(2):
            c, s = cos_ref[p : p + 1, at], sin_ref[p : p + 1, at]
            into[pl.ds(2 * p * nev, nev), :] = (c * vr - s * vi).astype(BF16)
            into[pl.ds((2 * p + 1) * nev, nev), :] = (c * vi + s * vr).astype(BF16)

    @pl.when(step == 0)
    def _():
        acc[...] = jnp.zeros_like(acc)

    turn(0, turned[0])
    for j in range(span // sub):
        if (j + 1) * sub < span:
            turn(j + 1, turned[(j + 1) % 2])
        w = v_ref[0, :, 0, :, pl.ds(j * sub, sub)].reshape(2 * nev, sub)
        acc[...] += cols_dot(w, turned[j % 2][...])

    @pl.when(step == pl.num_programs(0) - 1)
    def _():
        for p in range(2):
            a, b, c = 2 * p * nev, (2 * p + 1) * nev, (2 * p + 2) * nev
            flat[pl.ds(a, nev), :] = (acc[:nev, a:b] + acc[nev:, b:c]) * scale
            flat[pl.ds(b, nev), :] = (acc[:nev, b:c] - acc[nev:, a:b]) * scale
        rows = 4 * nev // shares
        for k, out in enumerate(outs):
            share = lax.rem(here_ref[0] + k, shares)
            out[...] = flat[pl.ds(pl.multiple_of(share * rows, 16), rows), :].astype(out.dtype)


def elemental_shares(v, cosine, sine, here, shares, local, scale):
    _, _, colours, nev, sites = v.shape
    span = min(sites, 4096)
    sub = min(span, 1024)
    per = sites // span
    rows = 4 * nev // shares
    phase = pl.BlockSpec((2, span), lambda i: (0, i % per))
    whole = pl.BlockSpec((rows, nev), lambda i: (0, 0))
    return pl.pallas_call(
        functools.partial(elemental_kernel, scale, sub, shares),
        grid=(colours * per,),
        in_specs=[
            pl.BlockSpec(memory_space=pltpu.SMEM),
            phase,
            phase,
            pl.BlockSpec((1, 2, 1, nev, span), lambda i: (local, 0, i // per, 0, i % per)),
        ],
        out_specs=[whole] * shares,
        out_shape=[jax.ShapeDtypeStruct((rows, nev), F32 if k == 0 else BF16) for k in range(shares)],
        scratch_shapes=[pltpu.VMEM((2 * nev, 4 * nev), F32), pltpu.VMEM((4 * nev, nev), F32)]
        + [pltpu.VMEM((4 * nev, sub), BF16)] * 2,
        compiler_params=pltpu.CompilerParams(vmem_limit_bytes=VMEM_LIMIT),
        cost_estimate=pl.CostEstimate(
            flops=2 * 8 * nev * nev * colours * sites,
            bytes_accessed=4 * nev * colours * sites,
            transcendentals=0,
        ),
        name="elementals",
    )(here, cosine, sine, v)


def box_kernel(known, shares, locals_, has_base, pair_ref, here_ref, perm_ref, sign_ref, *refs):
    sinks = refs[:known]
    pieces = refs[known : known + known * shares]
    refs = refs[known + known * shares :]
    tau_ref = refs[0]
    refs = refs[3:] if has_base else refs[1:]
    fwd_ref, bwd_ref, ts, tab = refs[:4]
    lx = refs[4:]
    step = pl.program_id(0)
    nev = pieces[0].shape[-1]
    rows = pieces[0].shape[0]
    spins = perm_ref.shape[1]
    dim = spins * nev
    wide = tab.shape[-1]
    left, right = (lx[0:3], lx[3:6]), (lx[6:9], lx[9:12])
    tR, tI = tau_ref.at[0, 0, 0], tau_ref.at[1, 0, 0]
    sink, source = pair_ref[0, step], pair_ref[1, step]

    @pl.when(step == 0)
    def _():
        tab[...] = jnp.zeros_like(tab)

    def fill(side, p, er, ei):
        both = er.astype(F32) + (ei.astype(F32) if side == 0 else -ei.astype(F32))
        at = pl.ds(p * nev, nev)
        for k, e in enumerate((er, ei, both.astype(BF16))):
            tab[side, k, 0, at, 0:nev] = e
            tab[side, k, 1, at, wide - nev : wide] = e

    for t in range(known):

        @pl.when(lax.rem(sink, locals_) == t)
        def _():
            base = (sink // locals_) * (4 * nev)
            for p in range(2):
                er, ei = (
                    sinks[t][pl.ds(pl.multiple_of(base + (2 * p + c) * nev, 64), nev), :] for c in range(2)
                )
                fill(0, p, er, ei)

        @pl.when(source == t)
        def _():
            flat = left[0][0]
            for k in range(shares):
                share = lax.rem(here_ref[0] - k + shares, shares)
                flat[pl.ds(pl.multiple_of(share * rows, 16), rows), 0:nev] = pieces[t * shares + k][...]
            for p in range(2):
                er, ei = (flat[pl.ds((2 * p + c) * nev, nev), 0:nev] for c in range(2))
                fill(1, p, er, ei)

    ts[...] = (tR[...].astype(F32) + tI[...].astype(F32)).astype(BF16)
    taus = (tR, tI, ts)
    for s in range(spins):
        to, sign = [], []
        for p in range(2):
            at = jnp.int32(0)
            for r in range(1, spins):
                at = jnp.where(perm_ref[p, r] == s, r, at)
            to.append(pl.ds(pl.multiple_of(at * nev, 64), nev))
            sign.append((2 * sign_ref[p, at] - 1).astype(F32) * (1.0 if s < spins // 2 else -1.0))
        start = s * nev
        form, at = (0, start) if start + wide <= dim else (1, start + nev - wide)
        p1, p2, p3 = (rows_dot(tab[0, k, form], taus[k][pl.ds(at, wide), :]) for k in range(3))
        re = p1 - p2
        im = p3 - p1 - p2
        for k, x in enumerate((re, im, re + im)):
            for p in range(2):
                left[p][k][to[p], :] = x[p * nev : (p + 1) * nev].astype(BF16)
        form, at = (0, start) if start % 128 == 0 else (1, start + nev - wide)
        p1, p2, p3 = (cols_dot(tab[1, k, form], taus[k][:, pl.ds(at, wide)]) for k in range(3))
        re = p1 + p2
        im = p1 - p2 - p3
        for k, x in enumerate((re, im, re + im)):
            for p in range(2):
                right[1 - p][k][to[p], :] = (x[p * nev : (p + 1) * nev] * sign[p]).astype(BF16)

    tile = 256
    column = lax.broadcasted_iota(jnp.int32, (1, dim), 1)
    weight = jnp.where(column < dim // 2, 1.0, -1.0).astype(F32) * (0.5 / math.sqrt(dim))
    for d, out in ((0, fwd_ref), (1, bwd_ref)):
        for n in range(0, dim, tile):
            cols = pl.ds(n, tile)
            p1, p2, p3 = (rows_dot(left[d][k][...], right[d][k][:, cols]) for k in range(3))
            re = p1 - p2
            im = p3 - p1 - p2
            for r in range(spins):
                w = weight[:, n : n + tile] * (2 * sign_ref[d, r] - 1).astype(F32)
                block = slice(r * nev, (r + 1) * nev)
                out[0, 0, 0, block, cols] = (re[block] * w).astype(BF16)
                out[1, 0, 0, block, cols] = (im[block] * w).astype(BF16)


def boxes(pairs, here, perm, sign, sinks, pieces, tau, base, locals_):
    known, shares = len(sinks), len(pieces[0])
    _, _, _, dim, _ = tau.shape
    nev = pieces[0][0].shape[-1]
    smem = pl.BlockSpec(memory_space=pltpu.SMEM)
    big = pl.BlockSpec((2, 1, 1, dim, dim), lambda i, pair: (0, pair[0, i], pair[1, i], 0, 0))
    keep = pl.BlockSpec(memory_space=pl.ANY)
    small = lambda x: pl.BlockSpec(x.shape, lambda i, pair: (0, 0))
    flat = list(sinks) + [x for piece in pieces for x in piece]
    has_base = base is not None
    operands = [pairs, here, perm, sign] + flat + [tau] + (list(base) if has_base else [])
    count = pairs.shape[1]
    shape = jax.ShapeDtypeStruct(tau.shape, BF16)
    return pl.pallas_call(
        functools.partial(box_kernel, known, shares, locals_, has_base),
        grid_spec=pltpu.PrefetchScalarGridSpec(
            num_scalar_prefetch=1,
            grid=(count,),
            in_specs=[smem] * 3 + [small(x) for x in flat] + [big] + ([keep, keep] if has_base else []),
            out_specs=[big, big],
            scratch_shapes=[pltpu.VMEM((dim, dim), BF16), pltpu.VMEM((2, 3, 2, 2 * nev, 256), BF16)]
            + [pltpu.VMEM((dim, dim), BF16)] * 12,
        ),
        out_shape=[shape, shape],
        input_output_aliases={len(operands) - 2: 0, len(operands) - 1: 1} if has_base else {},
        compiler_params=pltpu.CompilerParams(vmem_limit_bytes=VMEM_LIMIT),
        cost_estimate=pl.CostEstimate(
            flops=count * 2 * 2 * (4 * dim**3 + 8 * dim * dim * nev),
            bytes_accessed=count * 12 * dim * dim,
            transcendentals=0,
        ),
        name="boxes",
    )(*operands)


def on_device(columns, rings, eigenvectors, site_index, momenta, perambulators, spin_perm, spin_sign):
    locals_, _, _, colours, nev = eigenvectors.shape
    roots = columns // rings
    cosine, sine = phases(site_index, momenta)
    v = jnp.transpose(eigenvectors, (0, 1, 3, 4, 2))
    here = lax.axis_index("gx").astype(jnp.int32).reshape(1)
    sites = eigenvectors.shape[2] * rings
    scale = 0.5 / math.sqrt(colours * sites * nev)
    sinks, pieces = [], []
    shift = lambda k: [(i, (i + k) % rings) for i in range(rings)]
    spread = [
        ((plane * roots + i) * rings + z, (i * rings + z) * rings + plane)
        for plane in range(rings)
        for i in range(roots)
        for z in range(rings)
    ]
    for local in range(locals_):
        parts = elemental_shares(v, cosine, sine, here, rings, local, scale)
        total = parts[0]
        for k in range(1, rings):
            total = total + lax.ppermute(parts[k], "gx", shift(k)).astype(F32)
        share = total.astype(BF16)
        pieces.append([share] + [lax.ppermute(share, "gx", shift(k)) for k in range(1, rings)])
        moved = lax.ppermute(share, ("ta", "gx"), spread)
        sinks.append(lax.all_gather(moved, "ta", tiled=True))
    base = None
    source_count = perambulators.shape[2]
    sink_count = perambulators.shape[1]
    for local in range(locals_):
        new = [
            (s, t)
            for t in range(source_count)
            for s in range(sink_count)
            if max(s % locals_, t) == local
        ]
        pairs = jnp.asarray(np.array(new, np.int32).T)
        base = boxes(
            pairs, here, spin_perm, spin_sign, sinks[: local + 1], pieces[: local + 1], perambulators, base, locals_
        )
    return tuple(base)


def solution(mesh):
    return jax.shard_map(
        functools.partial(on_device, mesh.shape["ta"], mesh.shape["gx"]),
        mesh=mesh,
        in_specs=(
            P("ta", None, "gx", None, None),
            P("gx"),
            P(),
            P(None, "gx", "ta", None, None),
            P(),
            P(),
        ),
        out_specs=(P(None, "gx", "ta", None, None), P(None, "gx", "ta", None, None)),
        check_vma=False,
    )
```

```python
import functools
import math

import jax
import jax.numpy as jnp
import numpy as np
from jax import lax
from jax.experimental import pallas as pl
from jax.experimental.pallas import tpu as pltpu
from jax.sharding import PartitionSpec as P

F32, BF16 = jnp.float32, jnp.bfloat16
L = 32
VMEM_LIMIT = 58 * 2**20
BOTH_LAST = (((1,), (1,)), ((), ()))


def rows_dot(a, b):
    return jnp.dot(a, b, preferred_element_type=F32)


def cols_dot(a, b):
    return lax.dot_general(a, b, BOTH_LAST, preferred_element_type=F32)


def trig_rows(momenta_ref, sites_ref, trig_ref, dense):
    q = sites_ref[...]
    coords = (q // (L * L), (q // L) & (L - 1), q & (L - 1))
    lanes = q.shape[1]
    for p in range(2):
        dotted = sum(momenta_ref[p, axis] * coords[axis] for axis in range(3))
        angles = (dotted & (L - 1)).astype(F32) * (2.0 * math.pi / L)
        dense[p] = jnp.cos(angles)
        dense[2 + p] = jnp.sin(angles)
    for row in range(4):
        for at in range(q.shape[0]):
            trig_ref[row : row + 1, at * lanes : (at + 1) * lanes] = dense[row, at : at + 1, :]


def elemental_kernel(scale, sub, per, first, last, resumed, waits, *refs):
    refs = list(refs)
    take = refs.pop
    if first:
        momenta_ref, sites_ref, v_ref = take(0), take(0), take(0)
    else:
        trig_ref, v_ref = take(0), take(0)
    start = take(0) if resumed else None
    for _ in range(waits):
        take(0)
    outs = [take(0) for _ in range(2 if last else 1)]
    if first:
        trig_ref, dense = take(0), take(0)
    acc, flat = take(0), take(0)
    turned = refs
    step = pl.program_id(0)
    nev, span = v_ref.shape[3], v_ref.shape[4]

    @pl.when(step == 0)
    def _():
        acc[...] = jnp.zeros_like(acc) if start is None else start[...]
        if first:
            trig_rows(momenta_ref, sites_ref, trig_ref, dense)

    chunk = lax.rem(step, per) * span if first else 0

    def turn(j, into):
        at = pl.ds(j * sub, sub)
        by = pl.ds(pl.multiple_of(chunk + j * sub, sub), sub)
        vr = v_ref[0, 0, 0, :, at].astype(F32)
        vi = v_ref[0, 1, 0, :, at].astype(F32)
        for p in range(2):
            c, s = trig_ref[p : p + 1, by], trig_ref[2 + p : 3 + p, by]
            into[pl.ds(2 * p * nev, nev), :] = (c * vr - s * vi).astype(BF16)
            into[pl.ds((2 * p + 1) * nev, nev), :] = (c * vi + s * vr).astype(BF16)

    turn(0, turned[0])
    for j in range(span // sub):
        if (j + 1) * sub < span:
            turn(j + 1, turned[(j + 1) % 2])
        w = v_ref[0, :, 0, :, pl.ds(j * sub, sub)].reshape(2 * nev, sub)
        acc[...] += cols_dot(w, turned[j % 2][...])

    @pl.when(step == pl.num_programs(0) - 1)
    def _():
        if not last:
            outs[0][...] = acc[...]
            return
        for p in range(2):
            a, b, c = 2 * p * nev, (2 * p + 1) * nev, (2 * p + 2) * nev
            flat[pl.ds(a, nev), :] = (acc[:nev, a:b] + acc[nev:, b:c]) * scale
            flat[pl.ds(b, nev), :] = (acc[:nev, b:c] - acc[nev:, a:b]) * scale
        outs[0][...] = flat[...]
        outs[1][...] = flat[...].astype(BF16)


def elementals(v, local, scale, steps, trig=None, momenta=None, site_index=None, start=None, waits=()):
    _, _, colours, nev, sites = v.shape
    span = sites * colours // steps[2]
    per = sites // span
    sub = min(span, 1024)
    low, high = steps[0], steps[1]
    first, last = trig is None, high == steps[2]
    fixed = lambda *shape: pl.BlockSpec(shape, lambda i: (0,) * len(shape))
    block = pl.BlockSpec((1, 2, 1, nev, span), lambda i: (local, 0, (i + low) // per, 0, (i + low) % per))
    lanes = 128
    if first:
        operands = [momenta, site_index.reshape(-1, lanes), v]
        specs = [pl.BlockSpec(memory_space=pltpu.SMEM), fixed(sites // lanes, lanes), block]
    else:
        operands = [trig, v]
        specs = [pl.BlockSpec((4, span), lambda i: (0, (i + low) % per)), block]
    if start is not None:
        operands.append(start)
        specs.append(fixed(2 * nev, 4 * nev))
    operands += waits
    specs += [pl.BlockSpec(memory_space=pl.ANY)] * len(waits)
    if last:
        outs = [((4 * nev, nev), F32), ((4 * nev, nev), BF16)]
    else:
        outs = [((2 * nev, 4 * nev), F32)]
    if first:
        outs.append(((4, sites), F32))
    scratch = [pltpu.VMEM((4, sites // lanes, lanes), F32)] if first else []
    return pl.pallas_call(
        functools.partial(elemental_kernel, scale, sub, per, first, last, start is not None, len(waits)),
        grid=(high - low,),
        in_specs=specs,
        out_specs=[fixed(*shape) for shape, _ in outs],
        out_shape=[jax.ShapeDtypeStruct(shape, dtype) for shape, dtype in outs],
        scratch_shapes=scratch
        + [pltpu.VMEM((2 * nev, 4 * nev), F32), pltpu.VMEM((4 * nev, nev), F32)]
        + [pltpu.VMEM((4 * nev, sub), BF16)] * 2,
        compiler_params=pltpu.CompilerParams(vmem_limit_bytes=VMEM_LIMIT),
        cost_estimate=pl.CostEstimate(
            flops=(high - low) * 16 * nev * nev * span,
            bytes_accessed=(high - low) * 4 * nev * span,
            transcendentals=0,
        ),
        name="elementals",
    )(*operands)


def fill(tab, side, p, er, ei):
    nev, wide = er.shape[1], tab.shape[-1]
    both = er.astype(F32) + (ei.astype(F32) if side == 0 else -ei.astype(F32))
    at = pl.ds(p * nev, nev)
    for k, e in enumerate((er, ei, both.astype(BF16))):
        tab[side, k, 0, at, 0:nev] = e
        tab[side, k, 1, at, wide - nev : wide] = e


def fill_sink(tab, refs, locals_, sink, mine):
    nev = tab.shape[-2] // 2
    roots = len(refs[0])
    back = lax.rem(mine - sink // locals_ + roots, roots)
    for t, group in enumerate(refs):
        for m, ref in enumerate(group):

            @pl.when((lax.rem(sink, locals_) == t) & (back == m))
            def _():
                for p in range(2):
                    fill(tab, 0, p, *(ref[pl.ds((2 * p + c) * nev, nev), :] for c in range(2)))


def fill_source(tab, refs, source):
    nev = tab.shape[-2] // 2
    for t, ref in enumerate(refs):

        @pl.when(source == t)
        def _():
            for p in range(2):
                fill(tab, 1, p, *(ref[pl.ds((2 * p + c) * nev, nev), :] for c in range(2)))


def spin_places(perm_ref, sign_ref, p, s, nev):
    at = jnp.int32(0)
    for r in range(1, perm_ref.shape[1]):
        at = jnp.where(perm_ref[p, r] == s, r, at)
    return pl.ds(pl.multiple_of(at * nev, 64), nev), (2 * sign_ref[p, at] - 1).astype(F32)


def sum_parts(a, b):
    return (a.astype(F32) + b.astype(F32)).astype(BF16)


def left_rows(tab, taus, s, perm_ref, sign_ref, left):
    nev, wide = tab.shape[-2] // 2, tab.shape[-1]
    start = s * nev
    form, at = (0, start) if start + wide <= taus[0].shape[0] else (1, start + nev - wide)
    p1, p2, p3 = (rows_dot(tab[0, k, form], taus[k][pl.ds(at, wide), :]) for k in range(3))
    re = p1 - p2
    im = p3 - p1 - p2
    for p in range(2):
        to, _ = spin_places(perm_ref, sign_ref, p, s, nev)
        for k, x in enumerate((re, im, re + im)):
            left[p][k][to, :] = x[p * nev : (p + 1) * nev].astype(BF16)


def right_rows(tab, taus, s, perm_ref, sign_ref, right):
    nev, wide = tab.shape[-2] // 2, tab.shape[-1]
    start = s * nev
    form, at = (0, start) if start % 128 == 0 else (1, start + nev - wide)
    p1, p2, p3 = (cols_dot(tab[1, k, form], taus[k][:, pl.ds(at, wide)]) for k in range(3))
    re = p1 + p2
    im = p1 - p2 - p3
    for p in range(2):
        to, sign = spin_places(perm_ref, sign_ref, p, s, nev)
        sign = sign * (1.0 if s < perm_ref.shape[1] // 2 else -1.0)
        for k, x in enumerate((re, im, re + im)):
            right[1 - p][k][to, :] = (x[p * nev : (p + 1) * nev] * sign).astype(BF16)


def column_weight(dim):
    column = lax.broadcasted_iota(jnp.int32, (1, dim), 1)
    return jnp.where(column < dim // 2, 1.0, -1.0).astype(F32) * (0.5 / math.sqrt(dim))


def cut(refs, *counts):
    out, at = [], 0
    for count in counts:
        out.append(list(refs[at : at + count]))
        at += count
    return out + [list(refs[at:])]


TILE = 256


def full_kernel(levels, roots, sources, locals_, kept, pair_ref, here_ref, perm_ref, sign_ref, *refs):
    sinks, sources, (tau_ref,), _, (fwd_ref, bwd_ref, ts, tab), lx = cut(
        refs, levels * roots, sources, 1, kept, 4
    )
    step = pl.program_id(0)
    spins = perm_ref.shape[1]
    dim = tau_ref.shape[-1]
    nev = dim // spins
    left, right = (lx[0:3], lx[3:6]), (lx[6:9], lx[9:12])
    taus = (tau_ref.at[0, 0, 0], tau_ref.at[1, 0, 0], ts)

    @pl.when(step == 0)
    def _():
        tab[...] = jnp.zeros_like(tab)

    fill_sink(tab, cut(sinks, *[roots] * levels)[:-1], locals_, pair_ref[0, step], here_ref[1])
    fill_source(tab, sources, pair_ref[1, step])
    ts[...] = sum_parts(taus[0][...], taus[1][...])
    for s in range(spins):
        left_rows(tab, taus, s, perm_ref, sign_ref, left)
        right_rows(tab, taus, s, perm_ref, sign_ref, right)
    weight = column_weight(dim)
    for d, out in ((0, fwd_ref), (1, bwd_ref)):
        for n in range(0, dim, TILE):
            cols = pl.ds(n, TILE)
            p1, p2, p3 = (rows_dot(left[d][k][...], right[d][k][:, cols]) for k in range(3))
            re = p1 - p2
            im = p3 - p1 - p2
            for r in range(spins):
                w = weight[:, n : n + TILE] * (2 * sign_ref[d, r] - 1).astype(F32)
                block = slice(r * nev, (r + 1) * nev)
                out[0, 0, 0, block, cols] = (re[block] * w).astype(BF16)
                out[1, 0, 0, block, cols] = (im[block] * w).astype(BF16)


def inner_kernel(pair_ref, here_ref, perm_ref, sign_ref, source_ref, tau_ref, out_ref, ts, tab, *lx):
    step = pl.program_id(0)
    dim = tau_ref.shape[-1]
    right = (lx[0:3], lx[3:6])
    taus = (tau_ref.at[0, 0, 0], tau_ref.at[1, 0, 0], ts)

    @pl.when(step == 0)
    def _():
        tab[...] = jnp.zeros_like(tab)
        fill_source(tab, [source_ref], pair_ref[1, step])

    ts[...] = sum_parts(taus[0][...], taus[1][...])
    for s in range(perm_ref.shape[1]):
        right_rows(tab, taus, s, perm_ref, sign_ref, right)
    for d in range(2):
        for n in range(0, dim, TILE):
            cols = pl.ds(n, TILE)
            p1, p2, p3 = (rows_dot(taus[k][...], right[d][k][:, cols]) for k in range(3))
            out_ref[d, 0, 0, :, cols] = (p1 - p2).astype(BF16)
            out_ref[d, 1, 0, :, cols] = (p3 - p1 - p2).astype(BF16)


def outer_kernel(levels, roots, locals_, kept, pair_ref, here_ref, perm_ref, sign_ref, *refs):
    sinks, (inner_ref,), _, (fwd_ref, bwd_ref, ws, tab), _ = cut(refs, levels * roots, 1, kept, 4)
    step = pl.program_id(0)
    spins = perm_ref.shape[1]
    dim = inner_ref.shape[-1]
    nev, wide = dim // spins, tab.shape[-1]

    @pl.when(step == 0)
    def _():
        tab[...] = jnp.zeros_like(tab)

    fill_sink(tab, cut(sinks, *[roots] * levels)[:-1], locals_, pair_ref[0, step], here_ref[1])
    weight = column_weight(dim)
    for d, out in ((0, fwd_ref), (1, bwd_ref)):
        ws[d] = sum_parts(inner_ref[d, 0, 0], inner_ref[d, 1, 0])
        parts = (inner_ref.at[d, 0, 0], inner_ref.at[d, 1, 0], ws.at[d])
        for s in range(spins):
            start = s * nev
            form, at = (0, start) if start + wide <= dim else (1, start + nev - wide)
            mine = pl.ds(d * nev, nev)
            p1, p2, p3 = (rows_dot(tab[0, k, form, mine, :], parts[k][pl.ds(at, wide), :]) for k in range(3))
            to, sign = spin_places(perm_ref, sign_ref, d, s, nev)
            out[0, 0, 0, to, :] = ((p1 - p2) * (weight * sign)).astype(BF16)
            out[1, 0, 0, to, :] = ((p3 - p1 - p2) * (weight * sign)).astype(BF16)


def on_pairs(kernel, pairs, smalls, arrays, waits, base, out_shape, shape, out_block, in_blocks, scratch, nev, cost):
    pairs = jnp.asarray(np.array(pairs, np.int32).T)
    smem = pl.BlockSpec(memory_space=pltpu.SMEM)
    keep = pl.BlockSpec(memory_space=pl.ANY)
    scalars, wholes = smalls
    base = list(base) if base is not None else []
    operands = [pairs, *scalars, *wholes, *arrays, *waits, *base]
    dim = shape[-1]
    count = pairs.shape[1]
    outs = 1 if out_shape is not None else 2
    return pl.pallas_call(
        kernel,
        grid_spec=pltpu.PrefetchScalarGridSpec(
            num_scalar_prefetch=1,
            grid=(count,),
            in_specs=[smem] * len(scalars)
            + [pl.BlockSpec(x.shape, lambda i, pair: (0, 0)) for x in wholes]
            + in_blocks
            + [keep] * (len(waits) + len(base)),
            out_specs=[out_block] * outs,
            scratch_shapes=scratch,
        ),
        out_shape=[jax.ShapeDtypeStruct(out_shape or shape, BF16)] * outs,
        input_output_aliases={len(operands) - 2: 0, len(operands) - 1: 1} if base else {},
        compiler_params=pltpu.CompilerParams(vmem_limit_bytes=VMEM_LIMIT),
        cost_estimate=pl.CostEstimate(
            flops=count * cost, bytes_accessed=count * 12 * dim * dim, transcendentals=0
        ),
        name="boxes",
    )(*operands)


def pair_blocks(dim):
    return pl.BlockSpec((2, 1, 1, dim, dim), lambda i, pair: (0, pair[0, i], pair[1, i], 0, 0))


def full_boxes(pairs, scalars, sinks, sources, tau, waits, base, locals_, nev):
    dim = tau.shape[-1]
    square = pltpu.VMEM((dim, dim), BF16)
    table = pltpu.VMEM((2, 3, 2, 2 * nev, TILE), BF16)
    wholes = [x for group in sinks for x in group] + list(sources)
    kernel = functools.partial(
        full_kernel, len(sinks), len(sinks[0]), len(sources), locals_, len(waits) + (0 if base is None else 2)
    )
    cost = 4 * (3 * dim**3 + 6 * dim * dim * nev)
    return on_pairs(
        kernel, pairs, (scalars, wholes), [tau], waits, base, None, tau.shape,
        pair_blocks(dim), [pair_blocks(dim)], [square, table] + [square] * 12, nev, cost,
    )


def inner_boxes(pairs, scalars, source, tau, nev):
    dim = tau.shape[-1]
    square = pltpu.VMEM((dim, dim), BF16)
    table = pltpu.VMEM((2, 3, 2, 2 * nev, TILE), BF16)
    out_block = pl.BlockSpec((2, 2, 1, dim, dim), lambda i, pair: (0, 0, i, 0, 0))
    cost = 4 * (3 * dim**3 + 3 * dim * dim * nev)
    return on_pairs(
        inner_kernel, pairs, (scalars, [source]), [tau], [], None, (2, 2, len(pairs), dim, dim), tau.shape,
        out_block, [pair_blocks(dim)], [square, table] + [square] * 6, nev, cost,
    )[0]


def outer_boxes(pairs, scalars, sinks, inner, shape, base, locals_, nev):
    dim = shape[-1]
    table = pltpu.VMEM((2, 3, 2, 2 * nev, TILE), BF16)
    in_block = pl.BlockSpec((2, 2, 1, dim, dim), lambda i, pair: (0, 0, i, 0, 0))
    kernel = functools.partial(outer_kernel, len(sinks), len(sinks[0]), locals_, 0 if base is None else 2)
    cost = 12 * dim * dim * nev
    return on_pairs(
        kernel, pairs, (scalars, [x for group in sinks for x in group]), [inner], [], base, None, shape,
        pair_blocks(dim), [in_block], [pltpu.VMEM((2, dim, dim), BF16), table], nev, cost,
    )


def after(value, other):
    spot = lax.slice(other, (0,) * other.ndim, (1,) * other.ndim).reshape(1, 1).astype(F32)
    return (value.astype(F32) + 0.0 * spot).astype(value.dtype)


def on_device(columns, rings, eigenvectors, site_index, momenta, perambulators, spin_perm, spin_sign):
    locals_, _, sites, colours, nev = eigenvectors.shape
    roots = columns // rings
    v = jnp.transpose(eigenvectors, (0, 1, 3, 4, 2))
    here = jnp.stack([lax.axis_index("gx"), lax.rem(lax.axis_index("ta"), roots)]).astype(jnp.int32)
    scalars = [here, spin_perm, spin_sign]
    scale = 0.5 / math.sqrt(colours * sites * rings * nev)
    steps = colours * (sites // min(sites, 4096))
    stages = [1 << k for k in range(rings.bit_length() - 1)]
    spread = [
        ((plane * roots + i) * rings + z, (z * roots + i) * rings + plane)
        for plane in range(rings)
        for i in range(roots)
        for z in range(rings)
    ]
    tau = perambulators
    source_count, sink_count = tau.shape[2], tau.shape[1]
    last = locals_ - 1

    def exchange(x, bit):
        return lax.ppermute(x, "gx", [(i, i ^ bit) for i in range(rings)])

    def add(total, got):
        total = total + got.astype(F32)
        return total, total.astype(BF16)

    def spread_out(total):
        return lax.ppermute(total, ("ta", "gx"), spread)

    def gather_sinks(moved):
        found = [moved]
        for m in range(1, roots):
            pairs = [(g * roots + i, g * roots + (i + m) % roots) for g in range(rings) for i in range(roots)]
            found.append(lax.ppermute(moved, "ta", pairs))
        return found

    def pairs_of(level, source):
        return [(s, source) for s in range(sink_count) if s % locals_ == level and (level, source) != (last, 0)]

    total, sent, trig = elementals(v, 0, scale, (0, steps, steps), momenta=momenta, site_index=site_index)
    parts = []
    for local in range(1, locals_):
        bounds = [0, max(1, steps // 3), steps] if local == 1 and steps > 1 else [0, steps]
        parts += [(local, low, high) for low, high in zip(bounds, bounds[1:])]
    summed = {}

    def more_sums(wait):
        local, low, high = parts.pop(0)
        start = summed.get(local)
        summed[local] = elementals(
            v, local, scale, (low, high, steps), trig=trig, start=start and start[0], waits=[wait]
        )

    for bit in stages:
        got = exchange(sent, bit)
        if parts:
            more_sums(sent)
        total, sent = add(total, got)
    while parts:
        more_sums(sent)
    sources, moved = [sent], [spread_out(sent)]

    early = [(s, 0) for s in range(sink_count) if s % locals_ == last]
    inner = inner_boxes(early, scalars, sent, tau, nev)
    sinks, base, wait = [], None, inner
    for local in range(1, locals_):
        total, sent = summed[local]
        sent = after(total, sources[-1]).astype(BF16)
        for k, bit in enumerate(stages):
            got = exchange(sent, bit)
            if k == 1:
                if len(sinks) < local:
                    sinks.append(gather_sinks(after(moved[local - 1], wait)))
                new = [pair for level in range(local) for source in range(local) for pair in pairs_of(level, source)
                       if max(level, source) == local - 1]
                if new:
                    base = full_boxes(new, scalars, sinks, sources, tau, [sent, wait], base, locals_, nev)
                    wait = base[0]
            total, sent = add(after(total, wait), got)
        sources.append(sent)
        moved.append(spread_out(sent))
        new = [pair for level in range(local) for pair in pairs_of(level, local)] if len(sinks) == local else []
        if new:
            base = full_boxes(new, scalars, sinks, sources, tau, [wait] if base is None else [], base, locals_, nev)
            wait = base[0]
    sinks.append(gather_sinks(after(moved[last], wait)))
    new = [pair for source in range(source_count) for pair in pairs_of(last, source)]
    if new:
        base = full_boxes(new, scalars, sinks, sources, tau, [], base, locals_, nev)
    return tuple(outer_boxes(early, scalars, sinks, inner, tau.shape, base, locals_, nev))


def solution(mesh):
    return jax.shard_map(
        functools.partial(on_device, mesh.shape["ta"], mesh.shape["gx"]),
        mesh=mesh,
        in_specs=(
            P("ta", None, "gx", None, None),
            P("gx"),
            P(),
            P(None, "gx", "ta", None, None),
            P(),
            P(),
        ),
        out_specs=(P(None, "gx", "ta", None, None), P(None, "gx", "ta", None, None)),
        check_vma=False,
    )
```

```python
import functools
import math

import jax
import jax.numpy as jnp
import numpy as np
from jax import lax
from jax.experimental import pallas as pl
from jax.experimental.pallas import tpu as pltpu
from jax.sharding import PartitionSpec as P

F32, BF16 = jnp.float32, jnp.bfloat16
L = 32
VMEM_LIMIT = 58 * 2**20
BOTH_LAST = (((1,), (1,)), ((), ()))


def rows_dot(a, b):
    return jnp.dot(a, b, preferred_element_type=F32)


def cols_dot(a, b):
    return lax.dot_general(a, b, BOTH_LAST, preferred_element_type=F32)


def trig_rows(momenta_ref, sites_ref, trig_ref, dense):
    q = sites_ref[...]
    coords = (q // (L * L), (q // L) & (L - 1), q & (L - 1))
    lanes = q.shape[1]
    for p in range(2):
        dotted = sum(momenta_ref[p, axis] * coords[axis] for axis in range(3))
        angles = (dotted & (L - 1)).astype(F32) * (2.0 * math.pi / L)
        dense[p] = jnp.cos(angles)
        dense[2 + p] = jnp.sin(angles)
    for row in range(4):
        for at in range(q.shape[0]):
            trig_ref[row : row + 1, at * lanes : (at + 1) * lanes] = dense[row, at : at + 1, :]


def elemental_kernel(scale, sub, per, first, last, resumed, waits, *refs):
    refs = list(refs)
    take = refs.pop
    if first:
        momenta_ref, sites_ref, v_ref = take(0), take(0), take(0)
    else:
        trig_ref, v_ref = take(0), take(0)
    start = take(0) if resumed else None
    for _ in range(waits):
        take(0)
    outs = [take(0) for _ in range(2 if last else 1)]
    if first:
        trig_ref, dense = take(0), take(0)
    acc, flat = take(0), take(0)
    turned = refs
    step = pl.program_id(0)
    nev, span = v_ref.shape[3], v_ref.shape[4]

    @pl.when(step == 0)
    def _():
        acc[...] = jnp.zeros_like(acc) if start is None else start[...]
        if first:
            trig_rows(momenta_ref, sites_ref, trig_ref, dense)

    chunk = lax.rem(step, per) * span if first else 0

    def turn(j, into):
        at = pl.ds(j * sub, sub)
        by = pl.ds(pl.multiple_of(chunk + j * sub, sub), sub)
        vr = v_ref[0, 0, 0, :, at].astype(F32)
        vi = v_ref[0, 1, 0, :, at].astype(F32)
        for p in range(2):
            c, s = trig_ref[p : p + 1, by], trig_ref[2 + p : 3 + p, by]
            into[pl.ds(2 * p * nev, nev), :] = (c * vr - s * vi).astype(BF16)
            into[pl.ds((2 * p + 1) * nev, nev), :] = (c * vi + s * vr).astype(BF16)

    turn(0, turned[0])
    for j in range(span // sub):
        if (j + 1) * sub < span:
            turn(j + 1, turned[(j + 1) % 2])
        w = v_ref[0, :, 0, :, pl.ds(j * sub, sub)].reshape(2 * nev, sub)
        acc[...] += cols_dot(w, turned[j % 2][...])

    @pl.when(step == pl.num_programs(0) - 1)
    def _():
        if not last:
            outs[0][...] = acc[...]
            return
        for p in range(2):
            a, b, c = 2 * p * nev, (2 * p + 1) * nev, (2 * p + 2) * nev
            flat[pl.ds(a, nev), :] = (acc[:nev, a:b] + acc[nev:, b:c]) * scale
            flat[pl.ds(b, nev), :] = (acc[:nev, b:c] - acc[nev:, a:b]) * scale
        outs[0][...] = flat[...]
        outs[1][...] = flat[...].astype(BF16)


def elementals(v, local, scale, steps, trig=None, momenta=None, site_index=None, start=None, waits=()):
    _, _, colours, nev, sites = v.shape
    span = sites * colours // steps[2]
    per = sites // span
    sub = min(span, 1024)
    low, high = steps[0], steps[1]
    first, last = trig is None, high == steps[2]
    fixed = lambda *shape: pl.BlockSpec(shape, lambda i: (0,) * len(shape))
    block = pl.BlockSpec((1, 2, 1, nev, span), lambda i: (local, 0, (i + low) // per, 0, (i + low) % per))
    lanes = 128
    if first:
        operands = [momenta, site_index.reshape(-1, lanes), v]
        specs = [pl.BlockSpec(memory_space=pltpu.SMEM), fixed(sites // lanes, lanes), block]
    else:
        operands = [trig, v]
        specs = [pl.BlockSpec((4, span), lambda i: (0, (i + low) % per)), block]
    if start is not None:
        operands.append(start)
        specs.append(fixed(2 * nev, 4 * nev))
    operands += waits
    specs += [pl.BlockSpec(memory_space=pl.ANY)] * len(waits)
    if last:
        outs = [((4 * nev, nev), F32), ((4 * nev, nev), BF16)]
    else:
        outs = [((2 * nev, 4 * nev), F32)]
    if first:
        outs.append(((4, sites), F32))
    scratch = [pltpu.VMEM((4, sites // lanes, lanes), F32)] if first else []
    return pl.pallas_call(
        functools.partial(elemental_kernel, scale, sub, per, first, last, start is not None, len(waits)),
        grid=(high - low,),
        in_specs=specs,
        out_specs=[fixed(*shape) for shape, _ in outs],
        out_shape=[jax.ShapeDtypeStruct(shape, dtype) for shape, dtype in outs],
        scratch_shapes=scratch
        + [pltpu.VMEM((2 * nev, 4 * nev), F32), pltpu.VMEM((4 * nev, nev), F32)]
        + [pltpu.VMEM((4 * nev, sub), BF16)] * 2,
        compiler_params=pltpu.CompilerParams(vmem_limit_bytes=VMEM_LIMIT),
        cost_estimate=pl.CostEstimate(
            flops=(high - low) * 16 * nev * nev * span,
            bytes_accessed=(high - low) * 4 * nev * span,
            transcendentals=0,
        ),
        name="elementals",
    )(*operands)


def fill(tab, side, p, er, ei):
    nev, wide = er.shape[1], tab.shape[-1]
    both = er.astype(F32) + (ei.astype(F32) if side == 0 else -ei.astype(F32))
    at = pl.ds(p * nev, nev)
    for k, e in enumerate((er, ei, both.astype(BF16))):
        tab[side, k, 0, at, 0:nev] = e
        tab[side, k, 1, at, wide - nev : wide] = e


def fill_sink(tab, refs, locals_, sink, mine):
    nev = tab.shape[-2] // 2
    roots = len(refs[0])
    back = lax.rem(mine - sink // locals_ + roots, roots)
    for t, group in enumerate(refs):
        for m, ref in enumerate(group):

            @pl.when((lax.rem(sink, locals_) == t) & (back == m))
            def _():
                for p in range(2):
                    fill(tab, 0, p, *(ref[pl.ds((2 * p + c) * nev, nev), :] for c in range(2)))


def fill_source(tab, refs, source):
    nev = tab.shape[-2] // 2
    for t, ref in enumerate(refs):

        @pl.when(source == t)
        def _():
            for p in range(2):
                fill(tab, 1, p, *(ref[pl.ds((2 * p + c) * nev, nev), :] for c in range(2)))


def spin_places(perm_ref, sign_ref, p, s, nev):
    at = jnp.int32(0)
    for r in range(1, perm_ref.shape[1]):
        at = jnp.where(perm_ref[p, r] == s, r, at)
    return pl.ds(pl.multiple_of(at * nev, 64), nev), (2 * sign_ref[p, at] - 1).astype(F32)


def sum_parts(a, b):
    return (a.astype(F32) + b.astype(F32)).astype(BF16)


def left_rows(tab, taus, s, perm_ref, sign_ref, left):
    nev, wide = tab.shape[-2] // 2, tab.shape[-1]
    start = s * nev
    form, at = (0, start) if start + wide <= taus[0].shape[0] else (1, start + nev - wide)
    p1, p2, p3 = (rows_dot(tab[0, k, form], taus[k][pl.ds(at, wide), :]) for k in range(3))
    re = p1 - p2
    im = p3 - p1 - p2
    for p in range(2):
        to, _ = spin_places(perm_ref, sign_ref, p, s, nev)
        for k, x in enumerate((re, im, re + im)):
            left[p][k][to, :] = x[p * nev : (p + 1) * nev].astype(BF16)


def right_rows(tab, taus, s, perm_ref, sign_ref, right):
    nev, wide = tab.shape[-2] // 2, tab.shape[-1]
    start = s * nev
    form, at = (0, start) if start % 128 == 0 else (1, start + nev - wide)
    p1, p2, p3 = (cols_dot(tab[1, k, form], taus[k][:, pl.ds(at, wide)]) for k in range(3))
    re = p1 + p2
    im = p1 - p2 - p3
    for p in range(2):
        to, sign = spin_places(perm_ref, sign_ref, p, s, nev)
        sign = sign * (1.0 if s < perm_ref.shape[1] // 2 else -1.0)
        for k, x in enumerate((re, im, re + im)):
            right[1 - p][k][to, :] = (x[p * nev : (p + 1) * nev] * sign).astype(BF16)


def column_weight(dim):
    column = lax.broadcasted_iota(jnp.int32, (1, dim), 1)
    return jnp.where(column < dim // 2, 1.0, -1.0).astype(F32) * (0.5 / math.sqrt(dim))


def cut(refs, *counts):
    out, at = [], 0
    for count in counts:
        out.append(list(refs[at : at + count]))
        at += count
    return out + [list(refs[at:])]


TILE = 256


def send_out(buf, d, n, out, sink, source, sem):
    cols = pl.ds(n, TILE)
    return pltpu.make_async_copy(buf.at[d, :, :, cols], out.at[:, sink, source, :, cols], sem.at[d, n // TILE])


def full_step(levels, locals_, sink, source, first, here_ref, perm_ref, sign_ref, sinks, sources, tau_ref, outs, ts, tab, buf, sem, lx):
    spins = perm_ref.shape[1]
    dim = tau_ref.shape[-1]
    nev = dim // spins
    left, right = (lx[0:3], lx[3:6]), (lx[6:9], lx[9:12])
    taus = (tau_ref.at[0, 0, 0], tau_ref.at[1, 0, 0], ts)
    fill_sink(tab, sinks, locals_, sink, here_ref[1])
    fill_source(tab, sources, source)
    ts[...] = sum_parts(taus[0][...], taus[1][...])
    for s in range(spins):
        left_rows(tab, taus, s, perm_ref, sign_ref, left)
        right_rows(tab, taus, s, perm_ref, sign_ref, right)
    weight = column_weight(dim)
    for d, out in enumerate(outs):
        for n in range(0, dim, TILE):
            cols = pl.ds(n, TILE)
            p1, p2, p3 = (rows_dot(left[d][k][...], right[d][k][:, cols]) for k in range(3))
            re = p1 - p2
            im = p3 - p1 - p2
            copy = send_out(buf, d, n, out, sink, source, sem)

            @pl.when(jnp.logical_not(first))
            def _():
                copy.wait()

            for r in range(spins):
                w = weight[:, n : n + TILE] * (2 * sign_ref[d, r] - 1).astype(F32)
                block = slice(r * nev, (r + 1) * nev)
                buf[d, 0, block, cols] = (re[block] * w).astype(BF16)
                buf[d, 1, block, cols] = (im[block] * w).astype(BF16)
            copy.start()


def outer_step(locals_, sink, source, first, here_ref, perm_ref, sign_ref, sinks, inner_ref, outs, ws, tab, buf, sem):
    spins = perm_ref.shape[1]
    dim = inner_ref.shape[-1]
    nev, wide = dim // spins, tab.shape[-1]
    fill_sink(tab, sinks, locals_, sink, here_ref[1])
    weight = column_weight(dim)
    for d, out in enumerate(outs):
        copies = [send_out(buf, d, n, out, sink, source, sem) for n in range(0, dim, TILE)]

        @pl.when(jnp.logical_not(first))
        def _():
            for copy in copies:
                copy.wait()

        ws[...] = sum_parts(inner_ref[d, 0, 0], inner_ref[d, 1, 0])
        parts = (inner_ref.at[d, 0, 0], inner_ref.at[d, 1, 0], ws)
        mine = pl.ds(d * nev, nev)
        for s in range(spins):
            start = s * nev
            form, at = (0, start) if start + wide <= dim else (1, start + nev - wide)
            p1, p2, p3 = (rows_dot(tab[0, k, form, mine, :], parts[k][pl.ds(at, wide), :]) for k in range(3))
            to, sign = spin_places(perm_ref, sign_ref, d, s, nev)
            buf[d, 0, to, :] = ((p1 - p2) * (weight * sign)).astype(BF16)
            buf[d, 1, to, :] = ((p3 - p1 - p2) * (weight * sign)).astype(BF16)
        for copy in copies:
            copy.start()


def box_kernel(levels, roots, sources, locals_, has_full, has_outer, kept, pair_ref, here_ref, perm_ref, sign_ref, *refs):
    sinks, sources, tau, inner, _, outs, (token, tab, buf, sem), squares = cut(
        refs, levels * roots, sources, int(has_full), int(has_outer), kept, 2, 4
    )
    sinks = cut(sinks, *[roots] * levels)[:-1]
    step = pl.program_id(0)
    sink, source = pair_ref[0, step], pair_ref[1, step]
    first = step == 0

    @pl.when(first)
    def _():
        tab[...] = jnp.zeros_like(tab)
        token[...] = jnp.zeros_like(token)

    scalars = (here_ref, perm_ref, sign_ref)
    if has_full:

        @pl.when(pair_ref[2, step] == 0)
        def _():
            full_step(
                levels, locals_, sink, source, first, *scalars, sinks, sources, tau[0], outs,
                squares[0], tab, buf, sem, squares[1:13],
            )

    if has_outer:

        @pl.when(pair_ref[2, step] == 1)
        def _():
            outer_step(locals_, sink, source, first, *scalars, sinks, inner[0], outs, squares[0], tab, buf, sem)

    @pl.when(step == pl.num_programs(0) - 1)
    def _():
        for d, out in enumerate(outs):
            for n in range(0, buf.shape[-1], TILE):
                send_out(buf, d, n, out, sink, source, sem).wait()


def inner_kernel(pair_ref, here_ref, perm_ref, sign_ref, source_ref, tau_ref, out, token, tab, buf, sem, ts, *lx):
    step = pl.program_id(0)
    dim = tau_ref.shape[-1]
    right = (lx[0:3], lx[3:6])
    taus = (tau_ref.at[0, 0, 0], tau_ref.at[1, 0, 0], ts)

    @pl.when(step == 0)
    def _():
        tab[...] = jnp.zeros_like(tab)
        token[...] = jnp.zeros_like(token)
        fill_source(tab, [source_ref], pair_ref[1, step])

    ts[...] = sum_parts(taus[0][...], taus[1][...])
    for s in range(perm_ref.shape[1]):
        right_rows(tab, taus, s, perm_ref, sign_ref, right)

    def send(d, n):
        cols = pl.ds(n, TILE)
        return pltpu.make_async_copy(buf.at[d, :, :, cols], out.at[d, :, step, :, cols], sem.at[d, n // TILE])

    for d in range(2):
        for n in range(0, dim, TILE):
            cols = pl.ds(n, TILE)
            p1, p2, p3 = (rows_dot(taus[k][...], right[d][k][:, cols]) for k in range(3))

            @pl.when(step > 0)
            def _():
                send(d, n).wait()

            buf[d, 0, :, cols] = (p1 - p2).astype(BF16)
            buf[d, 1, :, cols] = (p3 - p1 - p2).astype(BF16)
            send(d, n).start()

    @pl.when(step == pl.num_programs(0) - 1)
    def _():
        for d in range(2):
            for n in range(0, dim, TILE):
                send(d, n).wait()


def on_pairs(kernel, pairs, scalars, wholes, arrays, blocks, waits, base, shapes, squares, nev, cost):
    pairs = jnp.asarray(np.array(pairs, np.int32).T)
    smem = pl.BlockSpec(memory_space=pltpu.SMEM)
    keep = pl.BlockSpec(memory_space=pl.ANY)
    base = list(base) if base is not None else []
    operands = [pairs, *scalars, *wholes, *arrays, *waits, *base]
    dim = shapes[0][-1]
    count = pairs.shape[1]
    return pl.pallas_call(
        kernel,
        grid_spec=pltpu.PrefetchScalarGridSpec(
            num_scalar_prefetch=1,
            grid=(count,),
            in_specs=[smem] * len(scalars)
            + [pl.BlockSpec(x.shape, lambda i, pair: (0, 0)) for x in wholes]
            + blocks
            + [keep] * (len(waits) + len(base)),
            out_specs=[keep] * len(shapes) + [pl.BlockSpec((1, nev), lambda i, pair: (0, 0))],
            scratch_shapes=[
                pltpu.VMEM((2, 3, 2, 2 * nev, TILE), BF16),
                pltpu.VMEM((2, 2, dim, dim), BF16),
                pltpu.SemaphoreType.DMA((2, dim // TILE)),
            ]
            + [pltpu.VMEM((dim, dim), BF16)] * squares,
        ),
        out_shape=[jax.ShapeDtypeStruct(shape, BF16) for shape in shapes] + [jax.ShapeDtypeStruct((1, nev), F32)],
        input_output_aliases={len(operands) - 2: 0, len(operands) - 1: 1} if base else {},
        compiler_params=pltpu.CompilerParams(vmem_limit_bytes=VMEM_LIMIT),
        cost_estimate=pl.CostEstimate(flops=cost, bytes_accessed=count * 12 * dim * dim, transcendentals=0),
        name="boxes",
    )(*operands)


def boxes(full, outer, scalars, sinks, sources, tau, inner, waits, base, locals_, nev):
    dim = tau.shape[-1]
    steps = [(s, t, 0) for s, t in full]
    if outer:
        steps[1:1] = [(s, t, 1) for s, t in outer]
    rows, pair, kept_inner = [], full[0] if full else (0, 0), 0
    for s, t, kind in steps:
        if kind == 0:
            pair = (s, t)
        else:
            kept_inner = outer.index((s, t))
        rows.append((s, t, kind, pair[0], pair[1], kept_inner))
    arrays, blocks = [], []
    if full:
        arrays.append(tau)
        blocks.append(pl.BlockSpec((2, 1, 1, dim, dim), lambda i, pair: (0, pair[3, i], pair[4, i], 0, 0)))
    if outer:
        arrays.append(inner)
        blocks.append(pl.BlockSpec((2, 2, 1, dim, dim), lambda i, pair: (0, 0, pair[5, i], 0, 0)))
    wholes = [x for group in sinks for x in group] + list(sources)
    kernel = functools.partial(
        box_kernel, len(sinks), len(sinks[0]), len(sources), locals_, bool(full), bool(outer),
        len(waits) + (0 if base is None else 2),
    )
    cost = 12 * len(full) * (dim**3 + 2 * dim * dim * nev) + 12 * len(outer) * dim * dim * nev
    out = on_pairs(
        kernel, rows, scalars, wholes, arrays, blocks, waits, base, [tau.shape] * 2, 13 if full else 1, nev, cost
    )
    return out[:2], out[2]


def inner_boxes(pairs, scalars, source, tau, nev):
    dim = tau.shape[-1]
    block = pl.BlockSpec((2, 1, 1, dim, dim), lambda i, pair: (0, pair[0, i], pair[1, i], 0, 0))
    cost = 12 * len(pairs) * (dim**3 + dim * dim * nev)
    return on_pairs(
        inner_kernel, pairs, scalars, [source], [tau], [block], [], None, [(2, 2, len(pairs), dim, dim)], 7, nev, cost
    )


def after(value, other):
    return (value.astype(F32) + 0.0 * other.astype(F32)).astype(value.dtype)


def on_device(columns, rings, eigenvectors, site_index, momenta, perambulators, spin_perm, spin_sign):
    locals_, _, sites, colours, nev = eigenvectors.shape
    roots = columns // rings
    v = jnp.transpose(eigenvectors, (0, 1, 3, 4, 2))
    here = jnp.stack([lax.axis_index("gx"), lax.rem(lax.axis_index("ta"), roots)]).astype(jnp.int32)
    scalars = [here, spin_perm, spin_sign]
    scale = 0.5 / math.sqrt(colours * sites * rings * nev)
    steps = colours * (sites // min(sites, 4096))
    stages = [1 << k for k in range(rings.bit_length() - 1)]
    spread = [
        ((plane * roots + i) * rings + z, ((z ^ plane) * roots + i) * rings + plane)
        for plane in range(rings)
        for i in range(roots)
        for z in range(rings)
    ]
    tau = perambulators
    source_count, sink_count = tau.shape[2], tau.shape[1]
    last = locals_ - 1

    def exchange(x, bit):
        return lax.ppermute(x, "gx", [(i, i ^ bit) for i in range(rings)])

    def add(total, got):
        total = total + got.astype(F32)
        return total, total.astype(BF16)

    def spread_out(total):
        return lax.ppermute(total, ("ta", "gx"), spread)

    def gather_sinks(moved):
        found = [moved]
        for m in range(1, roots):
            pairs = [(g * roots + i, g * roots + (i + m) % roots) for g in range(rings) for i in range(roots)]
            found.append(lax.ppermute(moved, "ta", pairs))
        return found

    def pairs_of(level, source):
        return [(s, source) for s in range(sink_count) if s % locals_ == level and (level, source) != (last, 0)]

    total, sent, trig = elementals(v, 0, scale, (0, steps, steps), momenta=momenta, site_index=site_index)
    parts = []
    for local in range(1, locals_):
        bounds = [0, max(1, steps // 3), steps] if local == 1 and steps > 1 else [0, steps]
        parts += [(local, low, high) for low, high in zip(bounds, bounds[1:])]
    summed = {}

    def more_sums(wait):
        local, low, high = parts.pop(0)
        start = summed.get(local)
        summed[local] = elementals(
            v, local, scale, (low, high, steps), trig=trig, start=start and start[0], waits=[wait]
        )

    for bit in stages:
        got = exchange(sent, bit)
        if parts:
            more_sums(sent)
        total, sent = add(total, got)
    while parts:
        more_sums(sent)
    sources, moved = [sent], [spread_out(sent)]

    early = [(s, 0) for s in range(sink_count) if s % locals_ == last]
    inner, wait = inner_boxes(early, scalars, sent, tau, nev)
    sinks, base = [], None
    for local in range(1, locals_):
        total, sent = summed[local]
        sent = after(total, sources[-1]).astype(BF16)
        for k, bit in enumerate(stages):
            got = exchange(sent, bit)
            if k == 1:
                if len(sinks) < local:
                    sinks.append(gather_sinks(after(moved[local - 1], wait)))
                new = [pair for level in range(local) for source in range(local) for pair in pairs_of(level, source)
                       if max(level, source) == local - 1]
                if new:
                    base, wait = boxes(new, [], scalars, sinks, sources, tau, None, [sent, wait], base, locals_, nev)
            total, sent = add(after(total, wait), got)
        sources.append(sent)
        moved.append(spread_out(sent))
        new = [pair for level in range(local) for pair in pairs_of(level, local)]
        if new:
            base, wait = boxes(new, [], scalars, sinks, sources, tau, None, [wait], base, locals_, nev)
    sinks.append(gather_sinks(after(moved[last], wait)))
    new = [pair for source in range(source_count) for pair in pairs_of(last, source)]
    base, _ = boxes(new, early, scalars, sinks, sources, tau, inner, [], base, locals_, nev)
    return tuple(base)


def solution(mesh):
    return jax.shard_map(
        functools.partial(on_device, mesh.shape["ta"], mesh.shape["gx"]),
        mesh=mesh,
        in_specs=(
            P("ta", None, "gx", None, None),
            P("gx"),
            P(),
            P(None, "gx", "ta", None, None),
            P(),
            P(),
        ),
        out_specs=(P(None, "gx", "ta", None, None), P(None, "gx", "ta", None, None)),
        check_vma=False,
    )
```

```python
import functools
import math

import jax
import jax.numpy as jnp
import numpy as np
from jax import lax
from jax.experimental import pallas as pl
from jax.experimental.pallas import tpu as pltpu
from jax.sharding import PartitionSpec as P

F32, BF16 = jnp.float32, jnp.bfloat16
L = 32
VMEM_LIMIT = 58 * 2**20
BOTH_LAST = (((1,), (1,)), ((), ()))


def rows_dot(a, b):
    return jnp.dot(a, b, preferred_element_type=F32)


def cols_dot(a, b):
    return lax.dot_general(a, b, BOTH_LAST, preferred_element_type=F32)


def trig_rows(momenta_ref, sites_ref, trig_ref, dense):
    q = sites_ref[...]
    coords = (q // (L * L), (q // L) & (L - 1), q & (L - 1))
    lanes = q.shape[1]
    for p in range(2):
        dotted = sum(momenta_ref[p, axis] * coords[axis] for axis in range(3))
        angles = (dotted & (L - 1)).astype(F32) * (2.0 * math.pi / L)
        dense[p] = jnp.cos(angles)
        dense[2 + p] = jnp.sin(angles)
    for row in range(4):
        for at in range(q.shape[0]):
            trig_ref[row : row + 1, at * lanes : (at + 1) * lanes] = dense[row, at : at + 1, :]


def elemental_kernel(scale, sub, per, first, last, resumed, waits, *refs):
    refs = list(refs)
    take = refs.pop
    if first:
        momenta_ref, sites_ref, v_ref = take(0), take(0), take(0)
    else:
        trig_ref, v_ref = take(0), take(0)
    start = take(0) if resumed else None
    for _ in range(waits):
        take(0)
    outs = [take(0) for _ in range(2 if last else 1)]
    if first:
        trig_ref, dense = take(0), take(0)
    acc, flat = take(0), take(0)
    turned = refs
    step = pl.program_id(0)
    nev, span = v_ref.shape[3], v_ref.shape[4]

    @pl.when(step == 0)
    def _():
        acc[...] = jnp.zeros_like(acc) if start is None else start[...]
        if first:
            trig_rows(momenta_ref, sites_ref, trig_ref, dense)

    chunk = lax.rem(step, per) * span if first else 0

    def turn(j, into):
        at = pl.ds(j * sub, sub)
        by = pl.ds(pl.multiple_of(chunk + j * sub, sub), sub)
        vr = v_ref[0, 0, 0, :, at].astype(F32)
        vi = v_ref[0, 1, 0, :, at].astype(F32)
        for p in range(2):
            c, s = trig_ref[p : p + 1, by], trig_ref[2 + p : 3 + p, by]
            into[pl.ds(2 * p * nev, nev), :] = (c * vr - s * vi).astype(BF16)
            into[pl.ds((2 * p + 1) * nev, nev), :] = (c * vi + s * vr).astype(BF16)

    turn(0, turned[0])
    for j in range(span // sub):
        if (j + 1) * sub < span:
            turn(j + 1, turned[(j + 1) % 2])
        w = v_ref[0, :, 0, :, pl.ds(j * sub, sub)].reshape(2 * nev, sub)
        acc[...] += cols_dot(w, turned[j % 2][...])

    @pl.when(step == pl.num_programs(0) - 1)
    def _():
        if not last:
            outs[0][...] = acc[...]
            return
        for p in range(2):
            a, b, c = 2 * p * nev, (2 * p + 1) * nev, (2 * p + 2) * nev
            flat[pl.ds(a, nev), :] = (acc[:nev, a:b] + acc[nev:, b:c]) * scale
            flat[pl.ds(b, nev), :] = (acc[:nev, b:c] - acc[nev:, a:b]) * scale
        outs[0][...] = flat[...]
        outs[1][...] = flat[...].astype(BF16)


def elementals(v, local, scale, steps, trig=None, momenta=None, site_index=None, start=None, waits=()):
    _, _, colours, nev, sites = v.shape
    span = sites * colours // steps[2]
    per = sites // span
    sub = min(span, 1024)
    low, high = steps[0], steps[1]
    first, last = trig is None, high == steps[2]
    fixed = lambda *shape: pl.BlockSpec(shape, lambda i: (0,) * len(shape))
    block = pl.BlockSpec((1, 2, 1, nev, span), lambda i: (local, 0, (i + low) // per, 0, (i + low) % per))
    lanes = 128
    if first:
        operands = [momenta, site_index.reshape(-1, lanes), v]
        specs = [pl.BlockSpec(memory_space=pltpu.SMEM), fixed(sites // lanes, lanes), block]
    else:
        operands = [trig, v]
        specs = [pl.BlockSpec((4, span), lambda i: (0, (i + low) % per)), block]
    if start is not None:
        operands.append(start)
        specs.append(fixed(2 * nev, 4 * nev))
    operands += waits
    specs += [pl.BlockSpec(memory_space=pl.ANY)] * len(waits)
    if last:
        outs = [((4 * nev, nev), F32), ((4 * nev, nev), BF16)]
    else:
        outs = [((2 * nev, 4 * nev), F32)]
    if first:
        outs.append(((4, sites), F32))
    scratch = [pltpu.VMEM((4, sites // lanes, lanes), F32)] if first else []
    return pl.pallas_call(
        functools.partial(elemental_kernel, scale, sub, per, first, last, start is not None, len(waits)),
        grid=(high - low,),
        in_specs=specs,
        out_specs=[fixed(*shape) for shape, _ in outs],
        out_shape=[jax.ShapeDtypeStruct(shape, dtype) for shape, dtype in outs],
        scratch_shapes=scratch
        + [pltpu.VMEM((2 * nev, 4 * nev), F32), pltpu.VMEM((4 * nev, nev), F32)]
        + [pltpu.VMEM((4 * nev, sub), BF16)] * 2,
        compiler_params=pltpu.CompilerParams(vmem_limit_bytes=VMEM_LIMIT),
        cost_estimate=pl.CostEstimate(
            flops=(high - low) * 16 * nev * nev * span,
            bytes_accessed=(high - low) * 4 * nev * span,
            transcendentals=0,
        ),
        name="elementals",
    )(*operands)


def fill(tab, side, p, er, ei):
    nev, wide = er.shape[1], tab.shape[-1]
    both = er.astype(F32) + (ei.astype(F32) if side == 0 else -ei.astype(F32))
    at = pl.ds(p * nev, nev)
    for k, e in enumerate((er, ei, both.astype(BF16))):
        tab[side, k, 0, at, 0:nev] = e
        tab[side, k, 1, at, wide - nev : wide] = e


def fill_sink(tab, refs, locals_, sink, mine):
    nev = tab.shape[-2] // 2
    roots = len(refs)
    back = lax.rem(mine - sink // locals_ + roots, roots)
    for m, ref in enumerate(refs):

        @pl.when(back == m)
        def _():
            for p in range(2):
                fill(tab, 0, p, *(ref[pl.ds((2 * p + c) * nev, nev), :] for c in range(2)))


def fill_source(tab, refs, source, first):
    nev = tab.shape[-2] // 2
    for t, ref in enumerate(refs):

        @pl.when(source == first + t)
        def _():
            for p in range(2):
                fill(tab, 1, p, *(ref[pl.ds((2 * p + c) * nev, nev), :] for c in range(2)))


def spin_places(perm_ref, sign_ref, p, s, nev):
    at = jnp.int32(0)
    for r in range(1, perm_ref.shape[1]):
        at = jnp.where(perm_ref[p, r] == s, r, at)
    return pl.ds(pl.multiple_of(at * nev, 64), nev), (2 * sign_ref[p, at] - 1).astype(F32)


def sum_parts(a, b):
    return (a.astype(F32) + b.astype(F32)).astype(BF16)


def left_rows(tab, taus, s, perm_ref, sign_ref, left):
    nev, wide = tab.shape[-2] // 2, tab.shape[-1]
    start = s * nev
    form, at = (0, start) if start + wide <= taus[0].shape[0] else (1, start + nev - wide)
    p1, p2, p3 = (rows_dot(tab[0, k, form], taus[k][pl.ds(at, wide), :]) for k in range(3))
    re = p1 - p2
    im = p3 - p1 - p2
    for p in range(2):
        to, _ = spin_places(perm_ref, sign_ref, p, s, nev)
        for k, x in enumerate((re, im, re + im)):
            left[p][k][to, :] = x[p * nev : (p + 1) * nev].astype(BF16)


def right_rows(tab, taus, s, perm_ref, sign_ref, right):
    nev, wide = tab.shape[-2] // 2, tab.shape[-1]
    start = s * nev
    form, at = (0, start) if start % 128 == 0 else (1, start + nev - wide)
    p1, p2, p3 = (cols_dot(tab[1, k, form], taus[k][:, pl.ds(at, wide)]) for k in range(3))
    re = p1 + p2
    im = p1 - p2 - p3
    for p in range(2):
        to, sign = spin_places(perm_ref, sign_ref, p, s, nev)
        sign = sign * (1.0 if s < perm_ref.shape[1] // 2 else -1.0)
        for k, x in enumerate((re, im, re + im)):
            right[1 - p][k][to, :] = (x[p * nev : (p + 1) * nev] * sign).astype(BF16)


def column_weight(dim):
    column = lax.broadcasted_iota(jnp.int32, (1, dim), 1)
    return jnp.where(column < dim // 2, 1.0, -1.0).astype(F32) * (0.5 / math.sqrt(dim))


def cut(refs, *counts):
    out, at = [], 0
    for count in counts:
        out.append(list(refs[at : at + count]))
        at += count
    return out + [list(refs[at:])]


TILE = 256


def full_step(locals_, sink, source, here_ref, perm_ref, sign_ref, sinks, sources, tau_ref, outs, ts, tab, lx):
    spins = perm_ref.shape[1]
    dim = tau_ref.shape[-1]
    nev = dim // spins
    left, right = (lx[0:3], lx[3:6]), (lx[6:9], lx[9:12])
    taus = (tau_ref.at[0, 0, 0], tau_ref.at[1, 0, 0], ts)
    fill_sink(tab, sinks, locals_, sink, here_ref[1])
    fill_source(tab, sources, source, 1)
    ts[...] = sum_parts(taus[0][...], taus[1][...])
    for s in range(spins):
        left_rows(tab, taus, s, perm_ref, sign_ref, left)
        right_rows(tab, taus, s, perm_ref, sign_ref, right)
    weight = column_weight(dim)
    for d, out in enumerate(outs):
        for n in range(0, dim, TILE):
            cols = pl.ds(n, TILE)
            p1, p2, p3 = (rows_dot(left[d][k][...], right[d][k][:, cols]) for k in range(3))
            re = p1 - p2
            im = p3 - p1 - p2
            for r in range(spins):
                w = weight[:, n : n + TILE] * (2 * sign_ref[d, r] - 1).astype(F32)
                block = slice(r * nev, (r + 1) * nev)
                out[0, 0, 0, block, cols] = (re[block] * w).astype(BF16)
                out[1, 0, 0, block, cols] = (im[block] * w).astype(BF16)


def outer_step(locals_, sink, here_ref, perm_ref, sign_ref, sinks, inner_ref, outs, ws, tab):
    spins = perm_ref.shape[1]
    dim = inner_ref.shape[-1]
    nev, wide = dim // spins, tab.shape[-1]
    fill_sink(tab, sinks, locals_, sink, here_ref[1])
    weight = column_weight(dim)
    for d, out in enumerate(outs):
        ws[...] = sum_parts(inner_ref[d, 0, 0], inner_ref[d, 1, 0])
        parts = (inner_ref.at[d, 0, 0], inner_ref.at[d, 1, 0], ws)
        mine = pl.ds(d * nev, nev)
        for s in range(spins):
            start = s * nev
            form, at = (0, start) if start + wide <= dim else (1, start + nev - wide)
            p1, p2, p3 = (rows_dot(tab[0, k, form, mine, :], parts[k][pl.ds(at, wide), :]) for k in range(3))
            to, sign = spin_places(perm_ref, sign_ref, d, s, nev)
            out[0, 0, 0, to, :] = ((p1 - p2) * (weight * sign)).astype(BF16)
            out[1, 0, 0, to, :] = ((p3 - p1 - p2) * (weight * sign)).astype(BF16)


def box_kernel(roots, sources, locals_, has_full, has_outer, kept, pair_ref, here_ref, perm_ref, sign_ref, *refs):
    sinks, sources, tau, inner, _, outs, (token, tab), squares = cut(
        refs, roots, sources, int(has_full), int(has_outer), kept, 2, 2
    )
    step = pl.program_id(0)
    sink, source = pair_ref[0, step], pair_ref[1, step]
    first = step == 0

    @pl.when(first)
    def _():
        tab[...] = jnp.zeros_like(tab)
        token[...] = jnp.zeros_like(token)

    scalars = (here_ref, perm_ref, sign_ref)
    if has_full:

        @pl.when(pair_ref[2, step] == 0)
        def _():
            full_step(
                locals_, sink, source, *scalars, sinks, sources, tau[0], outs, squares[0], tab, squares[1:]
            )

    if has_outer:

        @pl.when(pair_ref[2, step] == 1)
        def _():
            outer_step(locals_, sink, *scalars, sinks, inner[0], outs, squares[0], tab)


def inner_kernel(pair_ref, here_ref, perm_ref, sign_ref, source_ref, tau_ref, out, token, tab, ts, *lx):
    step = pl.program_id(0)
    dim = tau_ref.shape[-1]
    right = (lx[0:3], lx[3:6])
    taus = (tau_ref.at[0, 0, 0], tau_ref.at[1, 0, 0], ts)

    @pl.when(step == 0)
    def _():
        tab[...] = jnp.zeros_like(tab)
        token[...] = jnp.zeros_like(token)
        fill_source(tab, [source_ref], pair_ref[1, step], 0)

    ts[...] = sum_parts(taus[0][...], taus[1][...])
    for s in range(perm_ref.shape[1]):
        right_rows(tab, taus, s, perm_ref, sign_ref, right)

    for d in range(2):
        for n in range(0, dim, TILE):
            cols = pl.ds(n, TILE)
            p1, p2, p3 = (rows_dot(taus[k][...], right[d][k][:, cols]) for k in range(3))
            out[d, 0, 0, :, cols] = (p1 - p2).astype(BF16)
            out[d, 1, 0, :, cols] = (p3 - p1 - p2).astype(BF16)


def on_pairs(kernel, pairs, scalars, wholes, arrays, blocks, waits, base, shapes, out_block, squares, nev, cost):
    pairs = jnp.asarray(np.array(pairs, np.int32).T)
    smem = pl.BlockSpec(memory_space=pltpu.SMEM)
    keep = pl.BlockSpec(memory_space=pl.ANY)
    base = list(base) if base is not None else []
    operands = [pairs, *scalars, *wholes, *arrays, *waits, *base]
    dim = shapes[0][-1]
    count = pairs.shape[1]
    return pl.pallas_call(
        kernel,
        grid_spec=pltpu.PrefetchScalarGridSpec(
            num_scalar_prefetch=1,
            grid=(count,),
            in_specs=[smem] * len(scalars)
            + [pl.BlockSpec(x.shape, lambda i, pair: (0, 0)) for x in wholes]
            + blocks
            + [keep] * (len(waits) + len(base)),
            out_specs=[out_block] * len(shapes) + [pl.BlockSpec((1, nev), lambda i, pair: (0, 0))],
            scratch_shapes=[pltpu.VMEM((2, 3, 2, 2 * nev, TILE), BF16)]
            + [pltpu.VMEM((dim, dim), BF16)] * squares,
        ),
        out_shape=[jax.ShapeDtypeStruct(shape, BF16) for shape in shapes] + [jax.ShapeDtypeStruct((1, nev), F32)],
        input_output_aliases={len(operands) - 2: 0, len(operands) - 1: 1} if base else {},
        compiler_params=pltpu.CompilerParams(vmem_limit_bytes=VMEM_LIMIT),
        cost_estimate=pl.CostEstimate(flops=cost, bytes_accessed=count * 12 * dim * dim, transcendentals=0),
        name="boxes",
    )(*operands)


def boxes(full, outer, early, scalars, sinks, sources, tau, inner, waits, base, locals_, nev):
    dim = tau.shape[-1]
    steps = [(s, t, 0) for s, t in full]
    if outer:
        steps[1:1] = [(s, t, 1) for s, t in outer]
    rows, pair, kept_inner = [], full[0] if full else (0, 0), early.index(outer[0]) if outer else 0
    for s, t, kind in steps:
        if kind == 0:
            pair = (s, t)
        else:
            kept_inner = early.index((s, t))
        rows.append((s, t, kind, pair[0], pair[1], kept_inner))
    arrays, blocks = [], []
    if full:
        arrays.append(tau)
        blocks.append(pl.BlockSpec((2, 1, 1, dim, dim), lambda i, pair: (0, pair[3, i], pair[4, i], 0, 0)))
    if outer:
        arrays.append(inner)
        blocks.append(pl.BlockSpec((2, 2, 1, dim, dim), lambda i, pair: (0, 0, pair[5, i], 0, 0)))
    out_block = pl.BlockSpec((2, 1, 1, dim, dim), lambda i, pair: (0, pair[0, i], pair[1, i], 0, 0))
    wholes = list(sinks) + list(sources)
    kernel = functools.partial(
        box_kernel, len(sinks), len(sources), locals_, bool(full), bool(outer),
        len(waits) + (0 if base is None else 2),
    )
    cost = 12 * len(full) * (dim**3 + 2 * dim * dim * nev) + 12 * len(outer) * dim * dim * nev
    out = on_pairs(
        kernel, rows, scalars, wholes, arrays, blocks, waits, base, [tau.shape] * 2, out_block,
        13 if full else 1, nev, cost,
    )
    return out[:2], out[2]


def inner_boxes(pairs, scalars, source, tau, nev):
    dim = tau.shape[-1]
    block = pl.BlockSpec((2, 1, 1, dim, dim), lambda i, pair: (0, pair[0, i], pair[1, i], 0, 0))
    cost = 12 * len(pairs) * (dim**3 + dim * dim * nev)
    return on_pairs(
        inner_kernel, pairs, scalars, [source], [tau], [block], [], None, [(2, 2, len(pairs), dim, dim)],
        pl.BlockSpec((2, 2, 1, dim, dim), lambda i, pair: (0, 0, i, 0, 0)), 7, nev, cost,
    )


def after(value, other):
    return (value.astype(F32) + 0.0 * other.astype(F32)).astype(value.dtype)


def on_device(columns, rings, eigenvectors, site_index, momenta, perambulators, spin_perm, spin_sign):
    locals_, _, sites, colours, nev = eigenvectors.shape
    roots = columns // rings
    v = jnp.transpose(eigenvectors, (0, 1, 3, 4, 2))
    here = jnp.stack([lax.axis_index("gx"), lax.rem(lax.axis_index("ta"), roots)]).astype(jnp.int32)
    scalars = [here, spin_perm, spin_sign]
    scale = 0.5 / math.sqrt(colours * sites * rings * nev)
    steps = colours * (sites // min(sites, 4096))
    spread = [
        ((plane * roots + i) * rings + z, (z * roots + i) * rings + plane)
        for plane in range(rings)
        for i in range(roots)
        for z in range(rings)
    ]
    tau = perambulators
    source_count, sink_count = tau.shape[2], tau.shape[1]

    def exchange(sent):
        return [lax.ppermute(sent, "gx", [(i, i ^ k) for i in range(rings)]) for k in range(1, rings)]

    def add(total, got):
        for x in got:
            total = total + x.astype(F32)
        return total.astype(BF16)

    def spread_out(total):
        return lax.ppermute(total, ("ta", "gx"), spread)

    def gather_sinks(moved):
        found = [moved]
        for m in range(1, roots):
            pairs = [(g * roots + i, g * roots + (i + m) % roots) for g in range(rings) for i in range(roots)]
            found.append(lax.ppermute(moved, "ta", pairs))
        return found

    total, sent, trig = elementals(v, 0, scale, (0, steps, steps), momenta=momenta, site_index=site_index)
    got = exchange(sent)
    later = [elementals(v, local, scale, (0, steps, steps), trig=trig, waits=[sent]) for local in range(1, locals_)]
    sources = [add(total, got)]
    moved = [spread_out(sources[0])]
    sent = [after(total, sources[0]).astype(BF16) for total, _ in later]
    got = [exchange(x) for x in sent]

    early = [(s, 0) for s in range(sink_count)]
    inner, wait = inner_boxes(early, scalars, sources[0], tau, nev)
    for (total, _), x in zip(later, got):
        sources.append(add(after(total, wait), x))
        moved.append(spread_out(sources[-1]))
    base = None
    for level in range(locals_):
        sinks = gather_sinks(after(moved[level], wait))
        mine = [s for s in range(sink_count) if s % locals_ == level]
        full = [(s, t) for t in range(1, source_count) for s in mine]
        base, wait = boxes(
            full, [(s, 0) for s in mine], early, scalars, sinks, sources[1:], tau, inner, [], base, locals_, nev
        )
    return tuple(base)


def solution(mesh):
    return jax.shard_map(
        functools.partial(on_device, mesh.shape["ta"], mesh.shape["gx"]),
        mesh=mesh,
        in_specs=(
            P("ta", None, "gx", None, None),
            P("gx"),
            P(),
            P(None, "gx", "ta", None, None),
            P(),
            P(),
        ),
        out_specs=(P(None, "gx", "ta", None, None), P(None, "gx", "ta", None, None)),
        check_vma=False,
    )
```

```python
import functools
import math

import jax
import jax.numpy as jnp
import numpy as np
from jax import lax
from jax.experimental import pallas as pl
from jax.experimental.pallas import tpu as pltpu
from jax.sharding import PartitionSpec as P

F32, BF16 = jnp.float32, jnp.bfloat16
L = 32
VMEM_LIMIT = 58 * 2**20
BOTH_LAST = (((1,), (1,)), ((), ()))


def rows_dot(a, b):
    return jnp.dot(a, b, preferred_element_type=F32)


def cols_dot(a, b):
    return lax.dot_general(a, b, BOTH_LAST, preferred_element_type=F32)


def trig_rows(momenta_ref, sites_ref, trig_ref, dense):
    q = sites_ref[...]
    coords = (q // (L * L), (q // L) & (L - 1), q & (L - 1))
    lanes = q.shape[1]
    for p in range(2):
        dotted = sum(momenta_ref[p, axis] * coords[axis] for axis in range(3))
        angles = (dotted & (L - 1)).astype(F32) * (2.0 * math.pi / L)
        dense[p] = jnp.cos(angles)
        dense[2 + p] = jnp.sin(angles)
    for row in range(4):
        for at in range(q.shape[0]):
            trig_ref[row : row + 1, at * lanes : (at + 1) * lanes] = dense[row, at : at + 1, :]


def elemental_kernel(scale, sub, per, first, last, resumed, waits, *refs):
    refs = list(refs)
    take = refs.pop
    if first:
        momenta_ref, sites_ref, v_ref = take(0), take(0), take(0)
    else:
        trig_ref, v_ref = take(0), take(0)
    start = take(0) if resumed else None
    for _ in range(waits):
        take(0)
    outs = [take(0) for _ in range(2 if last else 1)]
    if first:
        trig_ref, dense = take(0), take(0)
    acc, flat = take(0), take(0)
    turned = refs
    step = pl.program_id(0)
    nev, span = v_ref.shape[3], v_ref.shape[4]

    @pl.when(step == 0)
    def _():
        acc[...] = jnp.zeros_like(acc) if start is None else start[...]
        if first:
            trig_rows(momenta_ref, sites_ref, trig_ref, dense)

    chunk = lax.rem(step, per) * span if first else 0

    def turn(j, into):
        at = pl.ds(j * sub, sub)
        by = pl.ds(pl.multiple_of(chunk + j * sub, sub), sub)
        vr = v_ref[0, 0, 0, :, at].astype(F32)
        vi = v_ref[0, 1, 0, :, at].astype(F32)
        for p in range(2):
            c, s = trig_ref[p : p + 1, by], trig_ref[2 + p : 3 + p, by]
            into[pl.ds(2 * p * nev, nev), :] = (c * vr - s * vi).astype(BF16)
            into[pl.ds((2 * p + 1) * nev, nev), :] = (c * vi + s * vr).astype(BF16)

    turn(0, turned[0])
    for j in range(span // sub):
        if (j + 1) * sub < span:
            turn(j + 1, turned[(j + 1) % 2])
        w = v_ref[0, :, 0, :, pl.ds(j * sub, sub)].reshape(2 * nev, sub)
        acc[...] += cols_dot(w, turned[j % 2][...])

    @pl.when(step == pl.num_programs(0) - 1)
    def _():
        if not last:
            outs[0][...] = acc[...]
            return
        for p in range(2):
            a, b, c = 2 * p * nev, (2 * p + 1) * nev, (2 * p + 2) * nev
            flat[pl.ds(a, nev), :] = (acc[:nev, a:b] + acc[nev:, b:c]) * scale
            flat[pl.ds(b, nev), :] = (acc[:nev, b:c] - acc[nev:, a:b]) * scale
        outs[0][...] = flat[...]
        outs[1][...] = flat[...].astype(BF16)


def elementals(v, local, scale, steps, trig=None, momenta=None, site_index=None, start=None, waits=()):
    _, _, colours, nev, sites = v.shape
    span = sites * colours // steps[2]
    per = sites // span
    sub = min(span, 1024)
    low, high = steps[0], steps[1]
    first, last = trig is None, high == steps[2]
    fixed = lambda *shape: pl.BlockSpec(shape, lambda i: (0,) * len(shape))
    block = pl.BlockSpec((1, 2, 1, nev, span), lambda i: (local, 0, (i + low) // per, 0, (i + low) % per))
    lanes = 128
    if first:
        operands = [momenta, site_index.reshape(-1, lanes), v]
        specs = [pl.BlockSpec(memory_space=pltpu.SMEM), fixed(sites // lanes, lanes), block]
    else:
        operands = [trig, v]
        specs = [pl.BlockSpec((4, span), lambda i: (0, (i + low) % per)), block]
    if start is not None:
        operands.append(start)
        specs.append(fixed(2 * nev, 4 * nev))
    operands += waits
    specs += [pl.BlockSpec(memory_space=pl.ANY)] * len(waits)
    if last:
        outs = [((4 * nev, nev), F32), ((4 * nev, nev), BF16)]
    else:
        outs = [((2 * nev, 4 * nev), F32)]
    if first:
        outs.append(((4, sites), F32))
    scratch = [pltpu.VMEM((4, sites // lanes, lanes), F32)] if first else []
    return pl.pallas_call(
        functools.partial(elemental_kernel, scale, sub, per, first, last, start is not None, len(waits)),
        grid=(high - low,),
        in_specs=specs,
        out_specs=[fixed(*shape) for shape, _ in outs],
        out_shape=[jax.ShapeDtypeStruct(shape, dtype) for shape, dtype in outs],
        scratch_shapes=scratch
        + [pltpu.VMEM((2 * nev, 4 * nev), F32), pltpu.VMEM((4 * nev, nev), F32)]
        + [pltpu.VMEM((4 * nev, sub), BF16)] * 2,
        compiler_params=pltpu.CompilerParams(vmem_limit_bytes=VMEM_LIMIT),
        cost_estimate=pl.CostEstimate(
            flops=(high - low) * 16 * nev * nev * span,
            bytes_accessed=(high - low) * 4 * nev * span,
            transcendentals=0,
        ),
        name="elementals",
    )(*operands)


def fill(tab, side, p, er, ei):
    nev, wide = er.shape[1], tab.shape[-1]
    both = er.astype(F32) + (ei.astype(F32) if side == 0 else -ei.astype(F32))
    at = pl.ds(p * nev, nev)
    for k, e in enumerate((er, ei, both.astype(BF16))):
        tab[side, k, 0, at, 0:nev] = e
        tab[side, k, 1, at, wide - nev : wide] = e


def fill_sink(tab, refs, locals_, sink, mine):
    nev = tab.shape[-2] // 2
    roots = len(refs)
    back = lax.rem(mine - sink // locals_ + roots, roots)
    for m, ref in enumerate(refs):

        @pl.when(back == m)
        def _():
            for p in range(2):
                fill(tab, 0, p, *(ref[pl.ds((2 * p + c) * nev, nev), :] for c in range(2)))


def fill_source(tab, refs, source, first):
    nev = tab.shape[-2] // 2
    for t, ref in enumerate(refs):

        @pl.when(source == first + t)
        def _():
            for p in range(2):
                fill(tab, 1, p, *(ref[pl.ds((2 * p + c) * nev, nev), :] for c in range(2)))


def spin_places(perm_ref, sign_ref, p, s, nev):
    at = jnp.int32(0)
    for r in range(1, perm_ref.shape[1]):
        at = jnp.where(perm_ref[p, r] == s, r, at)
    return pl.ds(pl.multiple_of(at * nev, 64), nev), (2 * sign_ref[p, at] - 1).astype(F32)


def sum_parts(a, b):
    return (a.astype(F32) + b.astype(F32)).astype(BF16)


def left_rows(tab, taus, s, perm_ref, sign_ref, left):
    nev, wide = tab.shape[-2] // 2, tab.shape[-1]
    start = s * nev
    form, at = (0, start) if start + wide <= taus[0].shape[0] else (1, start + nev - wide)
    p1, p2, p3 = (rows_dot(tab[0, k, form], taus[k][pl.ds(at, wide), :]) for k in range(3))
    re = p1 - p2
    im = p3 - p1 - p2
    for p in range(2):
        to, _ = spin_places(perm_ref, sign_ref, p, s, nev)
        for k, x in enumerate((re, im, re + im)):
            left[p][k][to, :] = x[p * nev : (p + 1) * nev].astype(BF16)


def right_rows(tab, taus, s, perm_ref, sign_ref, right):
    nev, wide = tab.shape[-2] // 2, tab.shape[-1]
    start = s * nev
    form, at = (0, start) if start % 128 == 0 else (1, start + nev - wide)
    p1, p2, p3 = (cols_dot(tab[1, k, form], taus[k][:, pl.ds(at, wide)]) for k in range(3))
    re = p1 + p2
    im = p1 - p2 - p3
    for p in range(2):
        to, sign = spin_places(perm_ref, sign_ref, p, s, nev)
        sign = sign * (1.0 if s < perm_ref.shape[1] // 2 else -1.0)
        for k, x in enumerate((re, im, re + im)):
            right[1 - p][k][to, :] = (x[p * nev : (p + 1) * nev] * sign).astype(BF16)


def column_weight(dim):
    column = lax.broadcasted_iota(jnp.int32, (1, dim), 1)
    return jnp.where(column < dim // 2, 1.0, -1.0).astype(F32) * (0.5 / math.sqrt(dim))


def cut(refs, *counts):
    out, at = [], 0
    for count in counts:
        out.append(list(refs[at : at + count]))
        at += count
    return out + [list(refs[at:])]


TILE = 256


def full_step(locals_, sink, source, here_ref, perm_ref, sign_ref, sinks, sources, tau_ref, outs, ts, tab, lx):
    spins = perm_ref.shape[1]
    dim = tau_ref.shape[-1]
    nev = dim // spins
    left, right = (lx[0:3], lx[3:6]), (lx[6:9], lx[9:12])
    taus = (tau_ref.at[0, 0, 0], tau_ref.at[1, 0, 0], ts)
    fill_sink(tab, sinks, locals_, sink, here_ref[1])
    fill_source(tab, sources, source, 1)
    ts[...] = sum_parts(taus[0][...], taus[1][...])
    for s in range(spins):
        left_rows(tab, taus, s, perm_ref, sign_ref, left)
        right_rows(tab, taus, s, perm_ref, sign_ref, right)
    weight = column_weight(dim)
    for d, out in enumerate(outs):
        for n in range(0, dim, TILE):
            cols = pl.ds(n, TILE)
            p1, p2, p3 = (rows_dot(left[d][k][...], right[d][k][:, cols]) for k in range(3))
            re = p1 - p2
            im = p3 - p1 - p2
            for r in range(spins):
                w = weight[:, n : n + TILE] * (2 * sign_ref[d, r] - 1).astype(F32)
                block = slice(r * nev, (r + 1) * nev)
                out[0, 0, 0, block, cols] = (re[block] * w).astype(BF16)
                out[1, 0, 0, block, cols] = (im[block] * w).astype(BF16)


def outer_step(locals_, sink, here_ref, perm_ref, sign_ref, sinks, inner_ref, outs, ws, tab):
    spins = perm_ref.shape[1]
    dim = inner_ref.shape[-1]
    nev, wide = dim // spins, tab.shape[-1]
    fill_sink(tab, sinks, locals_, sink, here_ref[1])
    weight = column_weight(dim)
    for d, out in enumerate(outs):
        ws[...] = sum_parts(inner_ref[d, 0, 0], inner_ref[d, 1, 0])
        parts = (inner_ref.at[d, 0, 0], inner_ref.at[d, 1, 0], ws)
        mine = pl.ds(d * nev, nev)
        for s in range(spins):
            start = s * nev
            form, at = (0, start) if start + wide <= dim else (1, start + nev - wide)
            p1, p2, p3 = (rows_dot(tab[0, k, form, mine, :], parts[k][pl.ds(at, wide), :]) for k in range(3))
            to, sign = spin_places(perm_ref, sign_ref, d, s, nev)
            out[0, 0, 0, to, :] = ((p1 - p2) * (weight * sign)).astype(BF16)
            out[1, 0, 0, to, :] = ((p3 - p1 - p2) * (weight * sign)).astype(BF16)


def box_kernel(roots, sources, locals_, has_full, has_outer, kept, pair_ref, here_ref, perm_ref, sign_ref, *refs):
    sinks, sources, tau, inner, _, outs, (token, tab), squares = cut(
        refs, roots, sources, int(has_full), int(has_outer), kept, 2, 2
    )
    step = pl.program_id(0)
    sink, source = pair_ref[0, step], pair_ref[1, step]
    first = step == 0

    @pl.when(first)
    def _():
        tab[...] = jnp.zeros_like(tab)
        token[...] = jnp.zeros_like(token)

    scalars = (here_ref, perm_ref, sign_ref)
    if has_full:

        @pl.when(pair_ref[2, step] == 0)
        def _():
            full_step(
                locals_, sink, source, *scalars, sinks, sources, tau[0], outs, squares[0], tab, squares[1:]
            )

    if has_outer:

        @pl.when(pair_ref[2, step] == 1)
        def _():
            outer_step(locals_, sink, *scalars, sinks, inner[0], outs, squares[0], tab)


def inner_kernel(pair_ref, here_ref, perm_ref, sign_ref, source_ref, tau_ref, out, token, tab, ts, *lx):
    step = pl.program_id(0)
    dim = tau_ref.shape[-1]
    right = (lx[0:3], lx[3:6])
    taus = (tau_ref.at[0, 0, 0], tau_ref.at[1, 0, 0], ts)

    @pl.when(step == 0)
    def _():
        tab[...] = jnp.zeros_like(tab)
        token[...] = jnp.zeros_like(token)
        fill_source(tab, [source_ref], pair_ref[1, step], 0)

    ts[...] = sum_parts(taus[0][...], taus[1][...])
    for s in range(perm_ref.shape[1]):
        right_rows(tab, taus, s, perm_ref, sign_ref, right)

    for d in range(2):
        for n in range(0, dim, TILE):
            cols = pl.ds(n, TILE)
            p1, p2, p3 = (rows_dot(taus[k][...], right[d][k][:, cols]) for k in range(3))
            out[d, 0, 0, :, cols] = (p1 - p2).astype(BF16)
            out[d, 1, 0, :, cols] = (p3 - p1 - p2).astype(BF16)


def on_pairs(kernel, pairs, scalars, wholes, arrays, blocks, waits, base, shapes, out_block, squares, nev, cost):
    pairs = jnp.asarray(np.array(pairs, np.int32).T)
    smem = pl.BlockSpec(memory_space=pltpu.SMEM)
    keep = pl.BlockSpec(memory_space=pl.ANY)
    base = list(base) if base is not None else []
    operands = [pairs, *scalars, *wholes, *arrays, *waits, *base]
    dim = shapes[0][-1]
    count = pairs.shape[1]
    return pl.pallas_call(
        kernel,
        grid_spec=pltpu.PrefetchScalarGridSpec(
            num_scalar_prefetch=1,
            grid=(count,),
            in_specs=[smem] * len(scalars)
            + [pl.BlockSpec(x.shape, lambda i, pair: (0, 0)) for x in wholes]
            + blocks
            + [keep] * (len(waits) + len(base)),
            out_specs=[out_block] * len(shapes) + [pl.BlockSpec((1, nev), lambda i, pair: (0, 0))],
            scratch_shapes=[pltpu.VMEM((2, 3, 2, 2 * nev, TILE), BF16)]
            + [pltpu.VMEM((dim, dim), BF16)] * squares,
        ),
        out_shape=[jax.ShapeDtypeStruct(shape, BF16) for shape in shapes] + [jax.ShapeDtypeStruct((1, nev), F32)],
        input_output_aliases={len(operands) - 2: 0, len(operands) - 1: 1} if base else {},
        compiler_params=pltpu.CompilerParams(vmem_limit_bytes=VMEM_LIMIT),
        cost_estimate=pl.CostEstimate(flops=cost, bytes_accessed=count * 12 * dim * dim, transcendentals=0),
        name="boxes",
    )(*operands)


def boxes(full, outer, early, scalars, sinks, sources, tau, inner, waits, base, locals_, nev):
    dim = tau.shape[-1]
    steps = [(s, t, 0) for s, t in full]
    if outer:
        last = [(s, t, 1) for s, t in outer]
        while last:
            steps.insert(min(len(steps), 2 * (len(outer) - len(last)) + 1), last.pop(0))
    rows, pair, kept_inner = [], full[0] if full else (0, 0), early.index(outer[0]) if outer else 0
    for s, t, kind in steps:
        if kind == 0:
            pair = (s, t)
        else:
            kept_inner = early.index((s, t))
        rows.append((s, t, kind, pair[0], pair[1], kept_inner))
    arrays, blocks = [], []
    if full:
        arrays.append(tau)
        blocks.append(pl.BlockSpec((2, 1, 1, dim, dim), lambda i, pair: (0, pair[3, i], pair[4, i], 0, 0)))
    if outer:
        arrays.append(inner)
        blocks.append(pl.BlockSpec((2, 2, 1, dim, dim), lambda i, pair: (0, 0, pair[5, i], 0, 0)))
    out_block = pl.BlockSpec((2, 1, 1, dim, dim), lambda i, pair: (0, pair[0, i], pair[1, i], 0, 0))
    wholes = list(sinks) + list(sources)
    kernel = functools.partial(
        box_kernel, len(sinks), len(sources), locals_, bool(full), bool(outer),
        len(waits) + (0 if base is None else 2),
    )
    cost = 12 * len(full) * (dim**3 + 2 * dim * dim * nev) + 12 * len(outer) * dim * dim * nev
    out = on_pairs(
        kernel, rows, scalars, wholes, arrays, blocks, waits, base, [tau.shape] * 2, out_block,
        13 if full else 1, nev, cost,
    )
    return out[:2], out[2]


def inner_boxes(pairs, scalars, source, tau, nev):
    dim = tau.shape[-1]
    block = pl.BlockSpec((2, 1, 1, dim, dim), lambda i, pair: (0, pair[0, i], pair[1, i], 0, 0))
    cost = 12 * len(pairs) * (dim**3 + dim * dim * nev)
    return on_pairs(
        inner_kernel, pairs, scalars, [source], [tau], [block], [], None, [(2, 2, len(pairs), dim, dim)],
        pl.BlockSpec((2, 2, 1, dim, dim), lambda i, pair: (0, 0, i, 0, 0)), 7, nev, cost,
    )


def after(value, other):
    return (value.astype(F32) + 0.0 * other.astype(F32)).astype(value.dtype)


def on_device(columns, rings, eigenvectors, site_index, momenta, perambulators, spin_perm, spin_sign):
    locals_, _, sites, colours, nev = eigenvectors.shape
    roots = columns // rings
    v = jnp.transpose(eigenvectors, (0, 1, 3, 4, 2))
    here = jnp.stack([lax.axis_index("gx"), lax.rem(lax.axis_index("ta"), roots)]).astype(jnp.int32)
    scalars = [here, spin_perm, spin_sign]
    scale = 0.5 / math.sqrt(colours * sites * rings * nev)
    steps = colours * (sites // min(sites, 4096))
    tau = perambulators
    source_count, sink_count = tau.shape[2], tau.shape[1]

    def exchange(sent):
        return [lax.ppermute(sent, "gx", [(i, i ^ k) for i in range(rings)]) for k in range(1, rings)]

    def add(total, got):
        for x in got:
            total = total + x.astype(F32)
        return total.astype(BF16)

    def spread_out(total):
        mine = lax.axis_index("ta") // roots == lax.axis_index("gx")
        found = [jnp.where(mine, total, 0).astype(BF16)]
        for odd in range(1, rings, 2):
            pairs = [
                ((g * roots + i) * rings + (g ^ away), ((g ^ (odd + away)) * roots + i) * rings + g)
                for g in range(rings)
                for i in range(roots)
                for away in range(2)
                if odd + away < rings
            ]
            found.append(lax.ppermute(total, ("ta", "gx"), pairs))
        return found

    def gather_sinks(parts, other):
        moved = after(sum(x.astype(F32) for x in parts), other).astype(BF16)
        found = [moved]
        for m in range(1, roots):
            pairs = [(g * roots + i, g * roots + (i + m) % roots) for g in range(rings) for i in range(roots)]
            found.append(lax.ppermute(moved, "ta", pairs))
        return found

    total, sent, trig = elementals(v, 0, scale, (0, steps, steps), momenta=momenta, site_index=site_index)
    parts = []
    for local in range(1, locals_):
        bounds = [0, max(1, steps // 3), steps] if local == 1 and steps > 1 else [0, steps]
        parts += [(local, low, high) for low, high in zip(bounds, bounds[1:])]
    summed = {}

    def more_sums(wait):
        local, low, high = parts.pop(0)
        start = summed.get(local)
        summed[local] = elementals(
            v, local, scale, (low, high, steps), trig=trig, start=start and start[0], waits=[wait]
        )

    for bit in (1 << k for k in range(rings.bit_length() - 1)):
        got = lax.ppermute(sent, "gx", [(i, i ^ bit) for i in range(rings)])
        if parts:
            more_sums(sent)
        total = total + got.astype(F32)
        sent = total.astype(BF16)
    while parts:
        more_sums(sent)
    later = [summed[local] for local in range(1, locals_)]
    sources = [sent]
    moved = [spread_out(sources[0])]
    sent = [after(total, sources[0]).astype(BF16) for total, _ in later]
    got = [exchange(x) for x in sent]

    early = [(s, 0) for s in range(sink_count)]
    inner, wait = inner_boxes(early, scalars, sources[0], tau, nev)
    for (total, _), x in zip(later, got):
        sources.append(add(after(total, wait), x))
        moved.append(spread_out(sources[-1]))
    base = None
    for level in range(locals_):
        sinks = gather_sinks(moved[level], wait)
        mine = [s for s in range(sink_count) if s % locals_ == level]
        full = [(s, t) for t in range(1, source_count) for s in mine]
        base, wait = boxes(
            full, [(s, 0) for s in mine], early, scalars, sinks, sources[1:], tau, inner, [], base, locals_, nev
        )
    return tuple(base)


def solution(mesh):
    return jax.shard_map(
        functools.partial(on_device, mesh.shape["ta"], mesh.shape["gx"]),
        mesh=mesh,
        in_specs=(
            P("ta", None, "gx", None, None),
            P("gx"),
            P(),
            P(None, "gx", "ta", None, None),
            P(),
            P(),
        ),
        out_specs=(P(None, "gx", "ta", None, None), P(None, "gx", "ta", None, None)),
        check_vma=False,
    )
```

```python
import functools
import math

import jax
import jax.numpy as jnp
import numpy as np
from jax import lax
from jax.experimental import pallas as pl
from jax.experimental.pallas import tpu as pltpu
from jax.sharding import PartitionSpec as P

F32, BF16 = jnp.float32, jnp.bfloat16
L = 32
VMEM_LIMIT = 58 * 2**20
BOX_VMEM = 46 * 2**20
BOTH_LAST = (((1,), (1,)), ((), ()))


def rows_dot(a, b):
    return jnp.dot(a, b, preferred_element_type=F32)


def cols_dot(a, b):
    return lax.dot_general(a, b, BOTH_LAST, preferred_element_type=F32)


def trig_rows(momenta_ref, sites_ref, trig_ref, dense):
    q = sites_ref[...]
    coords = (q // (L * L), (q // L) & (L - 1), q & (L - 1))
    lanes = q.shape[1]
    for p in range(2):
        dotted = sum(momenta_ref[p, axis] * coords[axis] for axis in range(3))
        angles = (dotted & (L - 1)).astype(F32) * (2.0 * math.pi / L)
        dense[p] = jnp.cos(angles)
        dense[2 + p] = jnp.sin(angles)
    for row in range(4):
        for at in range(q.shape[0]):
            trig_ref[row : row + 1, at * lanes : (at + 1) * lanes] = dense[row, at : at + 1, :]


def elemental_kernel(scale, sub, per, first, last, resumed, waits, *refs):
    refs = list(refs)
    take = refs.pop
    if first:
        momenta_ref, sites_ref, v_ref = take(0), take(0), take(0)
    else:
        trig_ref, v_ref = take(0), take(0)
    start = take(0) if resumed else None
    for _ in range(waits):
        take(0)
    outs = [take(0) for _ in range(2 if last else 1)]
    if first:
        trig_ref, dense = take(0), take(0)
    acc, flat = take(0), take(0)
    turned = refs
    step = pl.program_id(0)
    nev, span = v_ref.shape[3], v_ref.shape[4]

    @pl.when(step == 0)
    def _():
        acc[...] = jnp.zeros_like(acc) if start is None else start[...]
        if first:
            trig_rows(momenta_ref, sites_ref, trig_ref, dense)

    chunk = lax.rem(step, per) * span if first else 0

    def turn(j, into):
        at = pl.ds(j * sub, sub)
        by = pl.ds(pl.multiple_of(chunk + j * sub, sub), sub)
        vr = v_ref[0, 0, 0, :, at].astype(F32)
        vi = v_ref[0, 1, 0, :, at].astype(F32)
        for p in range(2):
            c, s = trig_ref[p : p + 1, by], trig_ref[2 + p : 3 + p, by]
            into[pl.ds(2 * p * nev, nev), :] = (c * vr - s * vi).astype(BF16)
            into[pl.ds((2 * p + 1) * nev, nev), :] = (c * vi + s * vr).astype(BF16)

    turn(0, turned[0])
    for j in range(span // sub):
        if (j + 1) * sub < span:
            turn(j + 1, turned[(j + 1) % 2])
        w = v_ref[0, :, 0, :, pl.ds(j * sub, sub)].reshape(2 * nev, sub)
        acc[...] += cols_dot(w, turned[j % 2][...])

    @pl.when(step == pl.num_programs(0) - 1)
    def _():
        if not last:
            outs[0][...] = acc[...]
            return
        for p in range(2):
            a, b, c = 2 * p * nev, (2 * p + 1) * nev, (2 * p + 2) * nev
            flat[pl.ds(a, nev), :] = (acc[:nev, a:b] + acc[nev:, b:c]) * scale
            flat[pl.ds(b, nev), :] = (acc[:nev, b:c] - acc[nev:, a:b]) * scale
        outs[0][...] = flat[...]
        outs[1][...] = flat[...].astype(BF16)


def elementals(v, local, scale, steps, trig=None, momenta=None, site_index=None, start=None, waits=()):
    _, _, colours, nev, sites = v.shape
    span = sites * colours // steps[2]
    per = sites // span
    sub = min(span, 1024)
    low, high = steps[0], steps[1]
    first, last = trig is None, high == steps[2]
    fixed = lambda *shape: pl.BlockSpec(shape, lambda i: (0,) * len(shape))
    block = pl.BlockSpec((1, 2, 1, nev, span), lambda i: (local, 0, (i + low) // per, 0, (i + low) % per))
    lanes = 128
    if first:
        operands = [momenta, site_index.reshape(-1, lanes), v]
        specs = [pl.BlockSpec(memory_space=pltpu.SMEM), fixed(sites // lanes, lanes), block]
    else:
        operands = [trig, v]
        specs = [pl.BlockSpec((4, span), lambda i: (0, (i + low) % per)), block]
    if start is not None:
        operands.append(start)
        specs.append(fixed(2 * nev, 4 * nev))
    operands += waits
    specs += [pl.BlockSpec(memory_space=pl.ANY)] * len(waits)
    if last:
        outs = [((4 * nev, nev), F32), ((4 * nev, nev), BF16)]
    else:
        outs = [((2 * nev, 4 * nev), F32)]
    if first:
        outs.append(((4, sites), F32))
    scratch = [pltpu.VMEM((4, sites // lanes, lanes), F32)] if first else []
    return pl.pallas_call(
        functools.partial(elemental_kernel, scale, sub, per, first, last, start is not None, len(waits)),
        grid=(high - low,),
        in_specs=specs,
        out_specs=[fixed(*shape) for shape, _ in outs],
        out_shape=[jax.ShapeDtypeStruct(shape, dtype) for shape, dtype in outs],
        scratch_shapes=scratch
        + [pltpu.VMEM((2 * nev, 4 * nev), F32), pltpu.VMEM((4 * nev, nev), F32)]
        + [pltpu.VMEM((4 * nev, sub), BF16)] * 2,
        compiler_params=pltpu.CompilerParams(vmem_limit_bytes=VMEM_LIMIT),
        cost_estimate=pl.CostEstimate(
            flops=(high - low) * 16 * nev * nev * span,
            bytes_accessed=(high - low) * 4 * nev * span,
            transcendentals=0,
        ),
        name="elementals",
    )(*operands)


def fill(tab, side, p, er, ei):
    nev, wide = er.shape[1], tab.shape[-1]
    both = er.astype(F32) + (ei.astype(F32) if side == 0 else -ei.astype(F32))
    at = pl.ds(p * nev, nev)
    for k, e in enumerate((er, ei, both.astype(BF16))):
        tab[side, k, 0, at, 0:nev] = e
        tab[side, k, 1, at, wide - nev : wide] = e


def fill_sink(tab, refs, locals_, sink, mine):
    nev = tab.shape[-2] // 2
    roots = len(refs)
    back = lax.rem(mine - sink // locals_ + roots, roots)
    for m, ref in enumerate(refs):

        @pl.when(back == m)
        def _():
            for p in range(2):
                fill(tab, 0, p, *(ref[pl.ds((2 * p + c) * nev, nev), :] for c in range(2)))


def fill_source(tab, refs, source, first):
    nev = tab.shape[-2] // 2
    for t, ref in enumerate(refs):

        @pl.when(source == first + t)
        def _():
            for p in range(2):
                fill(tab, 1, p, *(ref[pl.ds((2 * p + c) * nev, nev), :] for c in range(2)))


def spin_places(perm_ref, sign_ref, p, s, nev):
    at = jnp.int32(0)
    for r in range(1, perm_ref.shape[1]):
        at = jnp.where(perm_ref[p, r] == s, r, at)
    return pl.ds(pl.multiple_of(at * nev, 64), nev), (2 * sign_ref[p, at] - 1).astype(F32)


def sum_parts(a, b):
    return (a.astype(F32) + b.astype(F32)).astype(BF16)


def left_rows(tab, taus, s, perm_ref, sign_ref, left):
    nev, wide = tab.shape[-2] // 2, tab.shape[-1]
    start = s * nev
    form, at = (0, start) if start + wide <= taus[0].shape[0] else (1, start + nev - wide)
    for n in range(0, taus[0].shape[1], TILE):
        cols = pl.ds(n, TILE)
        p1, p2, p3 = (rows_dot(tab[0, k, form], taus[k][pl.ds(at, wide), cols]) for k in range(3))
        re = p1 - p2
        im = p3 - p1 - p2
        for p in range(2):
            to, _ = spin_places(perm_ref, sign_ref, p, s, nev)
            for k, x in enumerate((re, im, re + im)):
                left[p][k][to, cols] = x[p * nev : (p + 1) * nev].astype(BF16)


def right_rows(tab, taus, s, perm_ref, sign_ref, right):
    nev, wide = tab.shape[-2] // 2, tab.shape[-1]
    start = s * nev
    form, at = (0, start) if start % 128 == 0 else (1, start + nev - wide)
    for n in range(0, taus[0].shape[0], TILE):
        cols = pl.ds(n, TILE)
        p1, p2, p3 = (cols_dot(tab[1, k, form], taus[k][cols, pl.ds(at, wide)]) for k in range(3))
        re = p1 + p2
        im = p1 - p2 - p3
        for p in range(2):
            to, sign = spin_places(perm_ref, sign_ref, p, s, nev)
            sign = sign * (1.0 if s < perm_ref.shape[1] // 2 else -1.0)
            for k, x in enumerate((re, im, re + im)):
                right[1 - p][k][to, cols] = (x[p * nev : (p + 1) * nev] * sign).astype(BF16)


def column_weight(dim):
    column = lax.broadcasted_iota(jnp.int32, (1, dim), 1)
    return jnp.where(column < dim // 2, 1.0, -1.0).astype(F32) * (0.5 / math.sqrt(dim))


def cut(refs, *counts):
    out, at = [], 0
    for count in counts:
        out.append(list(refs[at : at + count]))
        at += count
    return out + [list(refs[at:])]


TILE = 256


def full_step(locals_, sink, source, here_ref, perm_ref, sign_ref, sinks, sources, tau_ref, outs, ts, tab, lx):
    spins = perm_ref.shape[1]
    dim = tau_ref.shape[-1]
    nev = dim // spins
    left, right = (lx[0:3], lx[3:6]), (lx[6:9], lx[9:12])
    taus = (tau_ref.at[0, 0, 0], tau_ref.at[1, 0, 0], ts)
    fill_sink(tab, sinks, locals_, sink, here_ref[0])
    fill_source(tab, sources, source, 1)
    ts[...] = sum_parts(taus[0][...], taus[1][...])
    for s in range(spins):
        left_rows(tab, taus, s, perm_ref, sign_ref, left)
        right_rows(tab, taus, s, perm_ref, sign_ref, right)
    weight = column_weight(dim)
    for d, out in enumerate(outs):
        for n in range(0, dim, TILE):
            cols = pl.ds(n, TILE)
            p1, p2, p3 = (rows_dot(left[d][k][...], right[d][k][:, cols]) for k in range(3))
            re = p1 - p2
            im = p3 - p1 - p2
            for r in range(spins):
                w = weight[:, n : n + TILE] * (2 * sign_ref[d, r] - 1).astype(F32)
                block = slice(r * nev, (r + 1) * nev)
                out[0, 0, 0, block, cols] = (re[block] * w).astype(BF16)
                out[1, 0, 0, block, cols] = (im[block] * w).astype(BF16)


def outer_step(locals_, sink, here_ref, perm_ref, sign_ref, sinks, inner_ref, outs, ws, tab):
    spins = perm_ref.shape[1]
    dim = inner_ref.shape[-1]
    nev, wide = dim // spins, tab.shape[-1]
    fill_sink(tab, sinks, locals_, sink, here_ref[0])
    weight = column_weight(dim)
    for d, out in enumerate(outs):
        ws[...] = sum_parts(inner_ref[d, 0, 0], inner_ref[d, 1, 0])
        parts = (inner_ref.at[d, 0, 0], inner_ref.at[d, 1, 0], ws)
        mine = pl.ds(d * nev, nev)
        for s in range(spins):
            start = s * nev
            form, at = (0, start) if start + wide <= dim else (1, start + nev - wide)
            to, sign = spin_places(perm_ref, sign_ref, d, s, nev)
            for n in range(0, dim, TILE):
                cols = pl.ds(n, TILE)
                p1, p2, p3 = (rows_dot(tab[0, k, form, mine, :], parts[k][pl.ds(at, wide), cols]) for k in range(3))
                w = weight[:, n : n + TILE] * sign
                out[0, 0, 0, to, cols] = ((p1 - p2) * w).astype(BF16)
                out[1, 0, 0, to, cols] = ((p3 - p1 - p2) * w).astype(BF16)


def box_kernel(roots, sources, locals_, has_full, has_outer, kept, pair_ref, here_ref, perm_ref, sign_ref, *refs):
    sinks, sources, tau, inner, _, outs, (token, tab), squares = cut(
        refs, roots, sources, int(has_full), int(has_outer), kept, 2, 2
    )
    step = pl.program_id(0)
    sink, source = pair_ref[0, step], pair_ref[1, step]
    first = step == 0

    @pl.when(first)
    def _():
        tab[...] = jnp.zeros_like(tab)
        token[...] = jnp.zeros_like(token)

    scalars = (here_ref, perm_ref, sign_ref)
    if has_full:

        @pl.when(pair_ref[2, step] == 0)
        def _():
            full_step(
                locals_, sink, source, *scalars, sinks, sources, tau[0], outs, squares[0], tab, squares[1:]
            )

    if has_outer:

        @pl.when(pair_ref[2, step] == 1)
        def _():
            outer_step(locals_, sink, *scalars, sinks, inner[0], outs, squares[0], tab)


def inner_kernel(pair_ref, here_ref, perm_ref, sign_ref, source_ref, tau_ref, out, token, tab, ts, *lx):
    step = pl.program_id(0)
    dim = tau_ref.shape[-1]
    right = (lx[0:3], lx[3:6])
    taus = (tau_ref.at[0, 0, 0], tau_ref.at[1, 0, 0], ts)

    @pl.when(step == 0)
    def _():
        tab[...] = jnp.zeros_like(tab)
        token[...] = jnp.zeros_like(token)
        fill_source(tab, [source_ref], pair_ref[1, step], 0)

    ts[...] = sum_parts(taus[0][...], taus[1][...])
    for s in range(perm_ref.shape[1]):
        right_rows(tab, taus, s, perm_ref, sign_ref, right)

    for d in range(2):
        for n in range(0, dim, TILE):
            cols = pl.ds(n, TILE)
            p1, p2, p3 = (rows_dot(taus[k][...], right[d][k][:, cols]) for k in range(3))
            out[d, 0, 0, :, cols] = (p1 - p2).astype(BF16)
            out[d, 1, 0, :, cols] = (p3 - p1 - p2).astype(BF16)


def on_pairs(kernel, pairs, scalars, wholes, arrays, blocks, waits, base, shapes, out_block, squares, nev, cost):
    pairs = jnp.asarray(np.array(pairs, np.int32).T)
    smem = pl.BlockSpec(memory_space=pltpu.SMEM)
    keep = pl.BlockSpec(memory_space=pl.ANY)
    base = list(base) if base is not None else []
    operands = [pairs, *scalars, *wholes, *arrays, *waits, *base]
    dim = shapes[0][-1]
    count = pairs.shape[1]
    return pl.pallas_call(
        kernel,
        grid_spec=pltpu.PrefetchScalarGridSpec(
            num_scalar_prefetch=1,
            grid=(count,),
            in_specs=[smem] * len(scalars)
            + [pl.BlockSpec(x.shape, lambda i, pair: (0, 0)) for x in wholes]
            + blocks
            + [keep] * (len(waits) + len(base)),
            out_specs=[out_block] * len(shapes) + [pl.BlockSpec((4 * nev, nev), lambda i, pair: (0, 0))],
            scratch_shapes=[pltpu.VMEM((2, 3, 2, 2 * nev, TILE), BF16)]
            + [pltpu.VMEM((dim, dim), BF16)] * squares,
        ),
        out_shape=[jax.ShapeDtypeStruct(shape, BF16) for shape in shapes] + [jax.ShapeDtypeStruct((4 * nev, nev), BF16)],
        input_output_aliases={len(operands) - 2: 0, len(operands) - 1: 1} if base else {},
        compiler_params=pltpu.CompilerParams(vmem_limit_bytes=BOX_VMEM),
        cost_estimate=pl.CostEstimate(flops=cost, bytes_accessed=count * 12 * dim * dim, transcendentals=0),
        name="boxes",
    )(*operands)


def boxes(full, outer, early, scalars, sinks, sources, tau, inner, waits, base, locals_, nev):
    dim = tau.shape[-1]
    steps = [(s, t, 0) for s, t in full]
    if outer:
        last = [(s, t, 1) for s, t in outer]
        while last:
            steps.insert(min(len(steps), 2 * (len(outer) - len(last)) + 1), last.pop(0))
    rows, pair, kept_inner = [], full[0] if full else (0, 0), early.index(outer[0]) if outer else 0
    for s, t, kind in steps:
        if kind == 0:
            pair = (s, t)
        else:
            kept_inner = early.index((s, t))
        rows.append((s, t, kind, pair[0], pair[1], kept_inner))
    arrays, blocks = [], []
    if full:
        arrays.append(tau)
        blocks.append(pl.BlockSpec((2, 1, 1, dim, dim), lambda i, pair: (0, pair[3, i], pair[4, i], 0, 0)))
    if outer:
        arrays.append(inner)
        blocks.append(pl.BlockSpec((2, 2, 1, dim, dim), lambda i, pair: (0, 0, pair[5, i], 0, 0)))
    out_block = pl.BlockSpec((2, 1, 1, dim, dim), lambda i, pair: (0, pair[0, i], pair[1, i], 0, 0))
    wholes = list(sinks) + list(sources)
    kernel = functools.partial(
        box_kernel, len(sinks), len(sources), locals_, bool(full), bool(outer),
        len(waits) + (0 if base is None else 2),
    )
    cost = 12 * len(full) * (dim**3 + 2 * dim * dim * nev) + 12 * len(outer) * dim * dim * nev
    out = on_pairs(
        kernel, rows, scalars, wholes, arrays, blocks, waits, base, [tau.shape] * 2, out_block,
        13 if full else 1, nev, cost,
    )
    return out[:2], out[2]


def inner_boxes(pairs, scalars, source, tau, nev):
    dim = tau.shape[-1]
    block = pl.BlockSpec((2, 1, 1, dim, dim), lambda i, pair: (0, pair[0, i], pair[1, i], 0, 0))
    cost = 12 * len(pairs) * (dim**3 + dim * dim * nev)
    return on_pairs(
        inner_kernel, pairs, scalars, [source], [tau], [block], [], None, [(2, 2, len(pairs), dim, dim)],
        pl.BlockSpec((2, 2, 1, dim, dim), lambda i, pair: (0, 0, i, 0, 0)), 7, nev, cost,
    )


def after(value, other):
    return (value.astype(F32) + 0.0 * other.astype(F32)).astype(value.dtype)


def on_device(columns, rings, eigenvectors, site_index, momenta, perambulators, spin_perm, spin_sign):
    locals_, _, sites, colours, nev = eigenvectors.shape
    roots = columns // rings
    v = jnp.transpose(eigenvectors, (0, 1, 3, 4, 2))
    here = lax.rem(lax.axis_index("ta"), roots).astype(jnp.int32).reshape(1)
    scalars = [here, spin_perm, spin_sign]
    scale = 0.5 / math.sqrt(colours * sites * rings * nev)
    steps = colours * (sites // min(sites, 4096))
    tau = perambulators
    source_count, sink_count = tau.shape[2], tau.shape[1]

    def exchange(sent):
        return [lax.ppermute(sent, "gx", [(i, i ^ k) for i in range(rings)]) for k in range(1, rings)]

    def add(total, got):
        for x in got:
            total = total + x.astype(F32)
        return total.astype(BF16)

    def spread_out(total):
        mine = lax.axis_index("ta") // roots == lax.axis_index("gx")
        found = [jnp.where(mine, total, 0).astype(BF16)]
        for odd in range(1, rings, 2):
            pairs = [
                ((g * roots + i) * rings + (g ^ away), ((g ^ (odd + away)) * roots + i) * rings + g)
                for g in range(rings)
                for i in range(roots)
                for away in range(2)
                if odd + away < rings
            ]
            found.append(lax.ppermute(total, ("ta", "gx"), pairs))
        return found

    def gather_sinks(parts, other):
        moved = after(sum(x.astype(F32) for x in parts), other).astype(BF16)
        found = [moved]
        for m in range(1, roots):
            pairs = [(g * roots + i, g * roots + (i + m) % roots) for g in range(rings) for i in range(roots)]
            found.append(lax.ppermute(moved, "ta", pairs))
        return found

    total, sent, trig = elementals(v, 0, scale, (0, steps, steps), momenta=momenta, site_index=site_index)
    parts = []
    for local in range(1, locals_):
        bounds = [0, max(1, steps // 3), steps] if local == 1 and steps > 1 else [0, steps]
        parts += [(local, low, high) for low, high in zip(bounds, bounds[1:])]
    summed = {}

    def more_sums(wait):
        local, low, high = parts.pop(0)
        start = summed.get(local)
        summed[local] = elementals(
            v, local, scale, (low, high, steps), trig=trig, start=start and start[0], waits=[wait]
        )

    for bit in (1 << k for k in range(rings.bit_length() - 1)):
        got = lax.ppermute(sent, "gx", [(i, i ^ bit) for i in range(rings)])
        if parts:
            more_sums(sent)
        total = total + got.astype(F32)
        sent = total.astype(BF16)
    while parts:
        more_sums(sent)
    later = [summed[local] for local in range(1, locals_)]
    sources = [sent]
    moved = [spread_out(sources[0])]
    sent = [after(total, sources[0]).astype(BF16) for total, _ in later]
    got = [exchange(x) for x in sent]

    early = [(s, 0) for s in range(sink_count)]
    inner, wait = inner_boxes(early, scalars, sources[0], tau, nev)
    for (total, _), x in zip(later, got):
        sources.append(add(after(total, wait), x))
        moved.append(spread_out(sources[-1]))
    base = None
    for level in range(locals_):
        sinks = gather_sinks(moved[level], wait)
        mine = [s for s in range(sink_count) if s % locals_ == level]
        full = [(s, t) for t in range(1, source_count) for s in mine]
        base, wait = boxes(
            full, [(s, 0) for s in mine], early, scalars, sinks, sources[1:], tau, inner, [], base, locals_, nev
        )
    return tuple(base)


def solution(mesh):
    return jax.shard_map(
        functools.partial(on_device, mesh.shape["ta"], mesh.shape["gx"]),
        mesh=mesh,
        in_specs=(
            P("ta", None, "gx", None, None),
            P("gx"),
            P(),
            P(None, "gx", "ta", None, None),
            P(),
            P(),
        ),
        out_specs=(P(None, "gx", "ta", None, None), P(None, "gx", "ta", None, None)),
        check_vma=False,
    )
```

```python
import functools
import math

import jax
import jax.numpy as jnp
import numpy as np
from jax import lax
from jax.experimental import pallas as pl
from jax.experimental.pallas import tpu as pltpu
from jax.sharding import PartitionSpec as P

F32, BF16 = jnp.float32, jnp.bfloat16
L = 32
VMEM_LIMIT = 58 * 2**20
BOX_VMEM = 46 * 2**20
BOTH_LAST = (((1,), (1,)), ((), ()))


def rows_dot(a, b):
    return jnp.dot(a, b, preferred_element_type=F32)


def cols_dot(a, b):
    return lax.dot_general(a, b, BOTH_LAST, preferred_element_type=F32)


def trig_rows(momenta_ref, sites_ref, trig_ref, dense):
    q = sites_ref[...]
    coords = (q // (L * L), (q // L) & (L - 1), q & (L - 1))
    lanes = q.shape[1]
    for p in range(2):
        dotted = sum(momenta_ref[p, axis] * coords[axis] for axis in range(3))
        angles = (dotted & (L - 1)).astype(F32) * (2.0 * math.pi / L)
        dense[p] = jnp.cos(angles)
        dense[2 + p] = jnp.sin(angles)
    for row in range(4):
        for at in range(q.shape[0]):
            trig_ref[row : row + 1, at * lanes : (at + 1) * lanes] = dense[row, at : at + 1, :]


def elemental_kernel(scale, sub, per, first, last, resumed, waits, *refs):
    refs = list(refs)
    take = refs.pop
    if first:
        momenta_ref, sites_ref, v_ref = take(0), take(0), take(0)
    else:
        trig_ref, v_ref = take(0), take(0)
    start = take(0) if resumed else None
    for _ in range(waits):
        take(0)
    outs = [take(0) for _ in range(2 if last else 1)]
    if first:
        trig_ref, dense = take(0), take(0)
    acc, flat = take(0), take(0)
    turned = refs
    step = pl.program_id(0)
    nev, span = v_ref.shape[3], v_ref.shape[4]

    @pl.when(step == 0)
    def _():
        acc[...] = jnp.zeros_like(acc) if start is None else start[...]
        if first:
            trig_rows(momenta_ref, sites_ref, trig_ref, dense)

    chunk = lax.rem(step, per) * span if first else 0

    def turn(j, into):
        at = pl.ds(j * sub, sub)
        by = pl.ds(pl.multiple_of(chunk + j * sub, sub), sub)
        vr = v_ref[0, 0, 0, :, at].astype(F32)
        vi = v_ref[0, 1, 0, :, at].astype(F32)
        for p in range(2):
            c, s = trig_ref[p : p + 1, by], trig_ref[2 + p : 3 + p, by]
            into[pl.ds(2 * p * nev, nev), :] = (c * vr - s * vi).astype(BF16)
            into[pl.ds((2 * p + 1) * nev, nev), :] = (c * vi + s * vr).astype(BF16)

    turn(0, turned[0])
    for j in range(span // sub):
        if (j + 1) * sub < span:
            turn(j + 1, turned[(j + 1) % 2])
        w = v_ref[0, :, 0, :, pl.ds(j * sub, sub)].reshape(2 * nev, sub)
        acc[...] += cols_dot(w, turned[j % 2][...])

    @pl.when(step == pl.num_programs(0) - 1)
    def _():
        if not last:
            outs[0][...] = acc[...]
            return
        for p in range(2):
            a, b, c = 2 * p * nev, (2 * p + 1) * nev, (2 * p + 2) * nev
            flat[pl.ds(a, nev), :] = (acc[:nev, a:b] + acc[nev:, b:c]) * scale
            flat[pl.ds(b, nev), :] = (acc[:nev, b:c] - acc[nev:, a:b]) * scale
        outs[0][...] = flat[...]
        outs[1][...] = flat[...].astype(BF16)


def elementals(v, local, scale, steps, trig=None, momenta=None, site_index=None, start=None, waits=()):
    _, _, colours, nev, sites = v.shape
    span = sites * colours // steps[2]
    per = sites // span
    sub = min(span, 1024)
    low, high = steps[0], steps[1]
    first, last = trig is None, high == steps[2]
    fixed = lambda *shape: pl.BlockSpec(shape, lambda i: (0,) * len(shape))
    block = pl.BlockSpec((1, 2, 1, nev, span), lambda i: (local, 0, (i + low) // per, 0, (i + low) % per))
    lanes = 128
    if first:
        operands = [momenta, site_index.reshape(-1, lanes), v]
        specs = [pl.BlockSpec(memory_space=pltpu.SMEM), fixed(sites // lanes, lanes), block]
    else:
        operands = [trig, v]
        specs = [pl.BlockSpec((4, span), lambda i: (0, (i + low) % per)), block]
    if start is not None:
        operands.append(start)
        specs.append(fixed(2 * nev, 4 * nev))
    operands += waits
    specs += [pl.BlockSpec(memory_space=pl.ANY)] * len(waits)
    if last:
        outs = [((4 * nev, nev), F32), ((4 * nev, nev), BF16)]
    else:
        outs = [((2 * nev, 4 * nev), F32)]
    if first:
        outs.append(((4, sites), F32))
    scratch = [pltpu.VMEM((4, sites // lanes, lanes), F32)] if first else []
    return pl.pallas_call(
        functools.partial(elemental_kernel, scale, sub, per, first, last, start is not None, len(waits)),
        grid=(high - low,),
        in_specs=specs,
        out_specs=[fixed(*shape) for shape, _ in outs],
        out_shape=[jax.ShapeDtypeStruct(shape, dtype) for shape, dtype in outs],
        scratch_shapes=scratch
        + [pltpu.VMEM((2 * nev, 4 * nev), F32), pltpu.VMEM((4 * nev, nev), F32)]
        + [pltpu.VMEM((4 * nev, sub), BF16)] * 2,
        compiler_params=pltpu.CompilerParams(vmem_limit_bytes=VMEM_LIMIT),
        cost_estimate=pl.CostEstimate(
            flops=(high - low) * 16 * nev * nev * span,
            bytes_accessed=(high - low) * 4 * nev * span,
            transcendentals=0,
        ),
        name="elementals",
    )(*operands)


def fill(tab, side, p, er, ei):
    nev, wide = er.shape[1], tab.shape[-1]
    both = er.astype(F32) + (ei.astype(F32) if side == 0 else -ei.astype(F32))
    at = pl.ds(p * nev, nev)
    for k, e in enumerate((er, ei, both.astype(BF16))):
        tab[side, k, 0, at, 0:nev] = e
        tab[side, k, 1, at, wide - nev : wide] = e


def fill_sink(tab, refs, locals_, sink, mine):
    nev = tab.shape[-2] // 2
    roots = len(refs)
    back = lax.rem(mine - sink // locals_ + roots, roots)
    for m, ref in enumerate(refs):

        @pl.when(back == m)
        def _():
            for p in range(2):
                fill(tab, 0, p, *(ref[pl.ds((2 * p + c) * nev, nev), :] for c in range(2)))


def fill_source(tab, refs, source, first):
    nev = tab.shape[-2] // 2
    for t, ref in enumerate(refs):

        @pl.when(source == first + t)
        def _():
            for p in range(2):
                fill(tab, 1, p, *(ref[pl.ds((2 * p + c) * nev, nev), :] for c in range(2)))


def spin_places(perm_ref, sign_ref, p, s, nev):
    at = jnp.int32(0)
    for r in range(1, perm_ref.shape[1]):
        at = jnp.where(perm_ref[p, r] == s, r, at)
    return pl.ds(pl.multiple_of(at * nev, 64), nev), (2 * sign_ref[p, at] - 1).astype(F32)


def sum_parts(a, b):
    return (a.astype(F32) + b.astype(F32)).astype(BF16)


def left_rows(tab, taus, s, perm_ref, sign_ref, left):
    nev, wide = tab.shape[-2] // 2, tab.shape[-1]
    start = s * nev
    form, at = (0, start) if start + wide <= taus[0].shape[0] else (1, start + nev - wide)
    for n in range(0, taus[0].shape[1], TILE):
        cols = pl.ds(n, TILE)
        p1, p2, p3 = (rows_dot(tab[0, k, form], taus[k][pl.ds(at, wide), cols]) for k in range(3))
        re = p1 - p2
        im = p3 - p1 - p2
        for p in range(2):
            to, _ = spin_places(perm_ref, sign_ref, p, s, nev)
            for k, x in enumerate((re, im, re + im)):
                left[p][k][to, cols] = x[p * nev : (p + 1) * nev].astype(BF16)


def right_rows(tab, taus, s, perm_ref, sign_ref, right):
    nev, wide = tab.shape[-2] // 2, tab.shape[-1]
    start = s * nev
    form, at = (0, start) if start % 128 == 0 else (1, start + nev - wide)
    for n in range(0, taus[0].shape[0], TILE):
        cols = pl.ds(n, TILE)
        p1, p2, p3 = (cols_dot(tab[1, k, form], taus[k][cols, pl.ds(at, wide)]) for k in range(3))
        re = p1 + p2
        im = p1 - p2 - p3
        for p in range(2):
            to, sign = spin_places(perm_ref, sign_ref, p, s, nev)
            sign = sign * (1.0 if s < perm_ref.shape[1] // 2 else -1.0)
            for k, x in enumerate((re, im, re + im)):
                right[1 - p][k][to, cols] = (x[p * nev : (p + 1) * nev] * sign).astype(BF16)


def column_weight(dim):
    column = lax.broadcasted_iota(jnp.int32, (1, dim), 1)
    return jnp.where(column < dim // 2, 1.0, -1.0).astype(F32) * (0.5 / math.sqrt(dim))


def cut(refs, *counts):
    out, at = [], 0
    for count in counts:
        out.append(list(refs[at : at + count]))
        at += count
    return out + [list(refs[at:])]


TILE = 256


def full_step(here_ref, perm_ref, sign_ref, tau_ref, outs, ts, tab, lx):
    spins = perm_ref.shape[1]
    dim = tau_ref.shape[-1]
    nev = dim // spins
    left, right = (lx[0:3], lx[3:6]), (lx[6:9], lx[9:12])
    taus = (tau_ref.at[0, 0, 0], tau_ref.at[1, 0, 0], ts)
    ts[...] = sum_parts(taus[0][...], taus[1][...])
    for s in range(spins):
        left_rows(tab, taus, s, perm_ref, sign_ref, left)
        right_rows(tab, taus, s, perm_ref, sign_ref, right)
    weight = column_weight(dim)
    for d, out in enumerate(outs):
        for n in range(0, dim, TILE):
            cols = pl.ds(n, TILE)
            p1, p2, p3 = (rows_dot(left[d][k][...], right[d][k][:, cols]) for k in range(3))
            re = p1 - p2
            im = p3 - p1 - p2
            for r in range(spins):
                w = weight[:, n : n + TILE] * (2 * sign_ref[d, r] - 1).astype(F32)
                block = slice(r * nev, (r + 1) * nev)
                out[0, 0, 0, block, cols] = (re[block] * w).astype(BF16)
                out[1, 0, 0, block, cols] = (im[block] * w).astype(BF16)


def outer_step(here_ref, perm_ref, sign_ref, inner_ref, outs, ws, tab):
    spins = perm_ref.shape[1]
    dim = inner_ref.shape[-1]
    nev, wide = dim // spins, tab.shape[-1]
    weight = column_weight(dim)
    for d, out in enumerate(outs):
        ws[d][...] = sum_parts(inner_ref[d, 0, 0], inner_ref[d, 1, 0])
        parts = (inner_ref.at[d, 0, 0], inner_ref.at[d, 1, 0], ws[d])
        mine = pl.ds(d * nev, nev)
        for s in range(spins):
            start = s * nev
            form, at = (0, start) if start + wide <= dim else (1, start + nev - wide)
            to, sign = spin_places(perm_ref, sign_ref, d, s, nev)
            for n in range(0, dim, TILE):
                cols = pl.ds(n, TILE)
                p1, p2, p3 = (rows_dot(tab[0, k, form, mine, :], parts[k][pl.ds(at, wide), cols]) for k in range(3))
                w = weight[:, n : n + TILE] * sign
                out[0, 0, 0, to, cols] = ((p1 - p2) * w).astype(BF16)
                out[1, 0, 0, to, cols] = ((p3 - p1 - p2) * w).astype(BF16)


def box_kernel(roots, sources, locals_, has_full, has_outer, kept, pair_ref, here_ref, perm_ref, sign_ref, *refs):
    sinks, sources, tau, inner, _, outs, (token, tab), squares = cut(
        refs, roots, sources, int(has_full), int(has_outer), kept, 2, 2
    )
    step = pl.program_id(0)
    first = step == 0
    before = jnp.maximum(step - 1, 0)
    sink, source = pair_ref[0, step], pair_ref[4, step]

    @pl.when(first)
    def _():
        tab[...] = jnp.zeros_like(tab)
        token[...] = jnp.zeros_like(token)

    scalars = (here_ref, perm_ref, sign_ref)

    @pl.when(first | (pair_ref[0, before] != sink))
    def _():
        fill_sink(tab, sinks, locals_, sink, here_ref[0])

    if has_full:

        @pl.when(first | (pair_ref[4, before] != source))
        def _():
            fill_source(tab, sources, source, 1)

        @pl.when(pair_ref[2, step] == 0)
        def _():
            full_step(*scalars, tau[0], outs, squares[0], tab, squares[1:])

    if has_outer:

        @pl.when(pair_ref[2, step] == 1)
        def _():
            outer_step(*scalars, inner[0], outs, squares[0:2], tab)


def inner_kernel(pair_ref, here_ref, perm_ref, sign_ref, source_ref, tau_ref, out, token, tab, ts, *lx):
    step = pl.program_id(0)
    dim = tau_ref.shape[-1]
    right = (lx[0:3], lx[3:6])
    taus = (tau_ref.at[0, 0, 0], tau_ref.at[1, 0, 0], ts)

    @pl.when(step == 0)
    def _():
        tab[...] = jnp.zeros_like(tab)
        token[...] = jnp.zeros_like(token)
        fill_source(tab, [source_ref], pair_ref[1, step], 0)

    ts[...] = sum_parts(taus[0][...], taus[1][...])
    for s in range(perm_ref.shape[1]):
        right_rows(tab, taus, s, perm_ref, sign_ref, right)

    for d in range(2):
        for n in range(0, dim, TILE):
            cols = pl.ds(n, TILE)
            p1, p2, p3 = (rows_dot(taus[k][...], right[d][k][:, cols]) for k in range(3))
            out[d, 0, 0, :, cols] = (p1 - p2).astype(BF16)
            out[d, 1, 0, :, cols] = (p3 - p1 - p2).astype(BF16)


def on_pairs(kernel, pairs, scalars, wholes, arrays, blocks, waits, base, shapes, out_block, squares, nev, cost):
    pairs = jnp.asarray(np.array(pairs, np.int32).T)
    smem = pl.BlockSpec(memory_space=pltpu.SMEM)
    keep = pl.BlockSpec(memory_space=pl.ANY)
    base = list(base) if base is not None else []
    operands = [pairs, *scalars, *wholes, *arrays, *waits, *base]
    dim = shapes[0][-1]
    count = pairs.shape[1]
    return pl.pallas_call(
        kernel,
        grid_spec=pltpu.PrefetchScalarGridSpec(
            num_scalar_prefetch=1,
            grid=(count,),
            in_specs=[smem] * len(scalars)
            + [pl.BlockSpec(x.shape, lambda i, pair: (0, 0)) for x in wholes]
            + blocks
            + [keep] * (len(waits) + len(base)),
            out_specs=[out_block] * len(shapes) + [pl.BlockSpec((4 * nev, nev), lambda i, pair: (0, 0))],
            scratch_shapes=[pltpu.VMEM((2, 3, 2, 2 * nev, TILE), BF16)]
            + [pltpu.VMEM((dim, dim), BF16)] * squares,
        ),
        out_shape=[jax.ShapeDtypeStruct(shape, BF16) for shape in shapes] + [jax.ShapeDtypeStruct((4 * nev, nev), BF16)],
        input_output_aliases={len(operands) - 2: 0, len(operands) - 1: 1} if base else {},
        compiler_params=pltpu.CompilerParams(vmem_limit_bytes=BOX_VMEM),
        cost_estimate=pl.CostEstimate(flops=cost, bytes_accessed=count * 12 * dim * dim, transcendentals=0),
        name="boxes",
    )(*operands)


def boxes(full, outer, early, scalars, sinks, sources, tau, inner, waits, base, locals_, nev):
    dim = tau.shape[-1]
    steps = [(s, t, 0) for s, t in full]
    if outer:
        last = [(s, t, 1) for s, t in outer]
        while last:
            steps.insert(min(len(steps), 2 * (len(outer) - len(last)) + 1), last.pop(0))
    rows, pair, kept_inner = [], full[0] if full else (0, 0), early.index(outer[0]) if outer else 0
    for s, t, kind in steps:
        if kind == 0:
            pair = (s, t)
        else:
            kept_inner = early.index((s, t))
        rows.append((s, t, kind, pair[0], pair[1], kept_inner))
    arrays, blocks = [], []
    if full:
        arrays.append(tau)
        blocks.append(pl.BlockSpec((2, 1, 1, dim, dim), lambda i, pair: (0, pair[3, i], pair[4, i], 0, 0)))
    if outer:
        arrays.append(inner)
        blocks.append(pl.BlockSpec((2, 2, 1, dim, dim), lambda i, pair: (0, 0, pair[5, i], 0, 0)))
    out_block = pl.BlockSpec((2, 1, 1, dim, dim), lambda i, pair: (0, pair[0, i], pair[1, i], 0, 0))
    wholes = list(sinks) + list(sources)
    kernel = functools.partial(
        box_kernel, len(sinks), len(sources), locals_, bool(full), bool(outer),
        len(waits) + (0 if base is None else 2),
    )
    cost = 12 * len(full) * (dim**3 + 2 * dim * dim * nev) + 12 * len(outer) * dim * dim * nev
    out = on_pairs(
        kernel, rows, scalars, wholes, arrays, blocks, waits, base, [tau.shape] * 2, out_block,
        13 if full else 2, nev, cost,
    )
    return out[:2], out[2]


def inner_boxes(pairs, scalars, source, tau, nev):
    dim = tau.shape[-1]
    block = pl.BlockSpec((2, 1, 1, dim, dim), lambda i, pair: (0, pair[0, i], pair[1, i], 0, 0))
    cost = 12 * len(pairs) * (dim**3 + dim * dim * nev)
    return on_pairs(
        inner_kernel, pairs, scalars, [source], [tau], [block], [], None, [(2, 2, len(pairs), dim, dim)],
        pl.BlockSpec((2, 2, 1, dim, dim), lambda i, pair: (0, 0, i, 0, 0)), 7, nev, cost,
    )


def after(value, other):
    return (value.astype(F32) + 0.0 * other.astype(F32)).astype(value.dtype)


def on_device(columns, rings, eigenvectors, site_index, momenta, perambulators, spin_perm, spin_sign):
    locals_, _, sites, colours, nev = eigenvectors.shape
    roots = columns // rings
    v = jnp.transpose(eigenvectors, (0, 1, 3, 4, 2))
    here = lax.rem(lax.axis_index("ta"), roots).astype(jnp.int32).reshape(1)
    scalars = [here, spin_perm, spin_sign]
    scale = 0.5 / math.sqrt(colours * sites * rings * nev)
    steps = colours * (sites // min(sites, 4096))
    tau = perambulators
    source_count, sink_count = tau.shape[2], tau.shape[1]

    def exchange(sent):
        return [lax.ppermute(sent, "gx", [(i, i ^ k) for i in range(rings)]) for k in range(1, rings)]

    def add(total, got):
        for x in got:
            total = total + x.astype(F32)
        return total.astype(BF16)

    def spread_out(total):
        mine = lax.axis_index("ta") // roots == lax.axis_index("gx")
        found = [jnp.where(mine, total, 0).astype(BF16)]
        for odd in range(1, rings, 2):
            pairs = [
                ((g * roots + i) * rings + (g ^ away), ((g ^ (odd + away)) * roots + i) * rings + g)
                for g in range(rings)
                for i in range(roots)
                for away in range(2)
                if odd + away < rings
            ]
            found.append(lax.ppermute(total, ("ta", "gx"), pairs))
        return found

    def gather_sinks(parts, other):
        moved = after(sum(x.astype(F32) for x in parts), other).astype(BF16)
        found = [moved]
        for m in range(1, roots):
            pairs = [(g * roots + i, g * roots + (i + m) % roots) for g in range(rings) for i in range(roots)]
            found.append(lax.ppermute(moved, "ta", pairs))
        return found

    total, sent, trig = elementals(v, 0, scale, (0, steps, steps), momenta=momenta, site_index=site_index)
    parts = []
    for local in range(1, locals_):
        bounds = [0, max(1, steps // 3), steps] if local == 1 and steps > 1 else [0, steps]
        parts += [(local, low, high) for low, high in zip(bounds, bounds[1:])]
    summed = {}

    def more_sums(wait):
        local, low, high = parts.pop(0)
        start = summed.get(local)
        summed[local] = elementals(
            v, local, scale, (low, high, steps), trig=trig, start=start and start[0], waits=[wait]
        )

    for bit in (1 << k for k in range(rings.bit_length() - 1)):
        got = lax.ppermute(sent, "gx", [(i, i ^ bit) for i in range(rings)])
        if parts:
            more_sums(sent)
        total = total + got.astype(F32)
        sent = total.astype(BF16)
    while parts:
        more_sums(sent)
    later = [summed[local] for local in range(1, locals_)]
    sources = [sent]
    moved = [spread_out(sources[0])]
    sent = [after(total, sources[0]).astype(BF16) for total, _ in later]
    got = [exchange(x) for x in sent]

    early = [(s, 0) for s in range(sink_count)]
    inner, wait = inner_boxes(early, scalars, sources[0], tau, nev)
    for (total, _), x in zip(later, got):
        sources.append(add(after(total, wait), x))
        moved.append(spread_out(sources[-1]))
    base = None
    for level in range(locals_):
        sinks = gather_sinks(moved[level], wait)
        mine = [s for s in range(sink_count) if s % locals_ == level]
        full = [(s, t) for t in range(1, source_count) for s in mine]
        base, wait = boxes(
            full, [(s, 0) for s in mine], early, scalars, sinks, sources[1:], tau, inner, [], base, locals_, nev
        )
    return tuple(base)


def solution(mesh):
    return jax.shard_map(
        functools.partial(on_device, mesh.shape["ta"], mesh.shape["gx"]),
        mesh=mesh,
        in_specs=(
            P("ta", None, "gx", None, None),
            P("gx"),
            P(),
            P(None, "gx", "ta", None, None),
            P(),
            P(),
        ),
        out_specs=(P(None, "gx", "ta", None, None), P(None, "gx", "ta", None, None)),
        check_vma=False,
    )
```
